512 devices in a mesh: tm: 16 (over z), tile: 32 (over x, y, core).
Axes of the slice: x: 4, y: 4, z: 16, core: 2. Of those that a mesh axis runs over, the one named last changes fastest.
Arguments:
- features: bfloat16 [64, 4, 256, 384], P('tm', None, 'tile'), may hold values from -500 to 500
- skip: bfloat16 [64, 4, 256, 384], P('tm', None, 'tile'), may hold values from -6 to 6
- norm_gain: float32 [384], replicated, may hold values from 0.1 to 1.9
- norm_bias: float32 [384], replicated, may hold values from -3 to 3
- conv_weight: bfloat16 [384, 27, 384], P('tm'), may hold values from -0.0625 to 0.0625
- conv_bias: float32 [384], replicated, may hold values from -3 to 3
- up_weight: bfloat16 [192, 9, 384], P('tm'), may hold values from -0.109375 to 0.109375
- up_bias: float32 [192], replicated, may hold values from -3 to 3
Outputs:
- upsampled: bfloat16 [64, 8, 512, 192], P('tm', None, 'tile')
The draws below stay inside these ranges and needn't reach their ends.
All inputs are finite; a program needn't handle non-finite values.
Results may differ from the reference program's by a relative error of at most 0.0051.
Values may be sent and summed in bfloat16 or wider, within the bound.
No kernel may reach another device: no remote copies, remote signals or barrier semaphores. Data moves between devices by JAX's collectives and lax.ppermute only.
A program may use at most 128 MiB of HBM per device.

```python
import jax
import jax.numpy as jnp
from jax import lax

CHANNELS = 384
OUT_CHANNELS = 192
GROUPS = 32
SLAB_ROWS = 4
COLS_DEV = 8
FRAMES = 64
COLUMNS = 256


def draw_features(key, part):
    key = jax.random.fold_in(key, 11)
    noise_key, chan_key, frame_key, offset_key, strip_key = jax.random.split(key, 5)
    shape = (FRAMES, SLAB_ROWS, COLUMNS, CHANNELS)
    strip_count = COLUMNS // COLS_DEV
    noise = jnp.clip(jax.random.normal(noise_key, shape, jnp.float32), -6.0, 6.0)
    strip_scale = jnp.exp(jax.random.uniform(strip_key, (FRAMES, strip_count), jnp.float32, jnp.log(0.1), jnp.log(10.0)))
    col_scale = jnp.repeat(strip_scale, COLS_DEV, axis=1)
    chan_scale = jnp.exp(jax.random.uniform(chan_key, (CHANNELS,), jnp.float32, jnp.log(0.3), jnp.log(3.0)))
    frame_scale = jnp.exp(jax.random.uniform(frame_key, (FRAMES,), jnp.float32, jnp.log(0.5), jnp.log(2.0)))
    offset = 0.7 * jnp.clip(jax.random.normal(offset_key, (FRAMES, 1, 1, CHANNELS), jnp.float32), -3.0, 3.0)
    return ((noise + offset) * frame_scale[:, None, None, None] * col_scale[:, None, :, None] * chan_scale).astype(jnp.bfloat16)


def level_of(key, shape, shards, low, top_value):
    loudness = 1.0
    for axis_at, shards_of in shards:
        heights = jax.random.uniform(jax.random.fold_in(jax.random.fold_in(key, 6), axis_at), (shards_of,), jnp.float32, low / len(shards), top_value / len(shards))
        loudness = loudness * jnp.repeat(jnp.exp(heights), shape[axis_at] // shards_of).reshape((-1,) + (1,) * (len(shape) - 1 - axis_at))
    return loudness


def gaussian(key, extent, scale, bound, cuts=(), kind=jnp.bfloat16):
    gain = level_of(key, extent, cuts, -0.22, 0.18) if cuts else 1.0
    drawn = jax.random.normal(key, extent, jnp.float32) * scale * gain
    return jnp.minimum(jnp.maximum(drawn, -bound), bound).astype(kind)


def setup_inputs(seed: int = 0) -> dict:
    key_of = jax.random.split(jax.random.key(seed), 9)
    return {
        "features": draw_features(jax.random.fold_in(key_of[8], 71), 0),
        "skip": gaussian(key_of[1], (FRAMES, SLAB_ROWS, COLUMNS, CHANNELS), 1.0, 6.0, ((0, 16), (2, 32))),
        "norm_gain": jnp.clip(1.0 + 0.18 * jax.random.normal(key_of[2], (CHANNELS,), jnp.float32), 0.1, 1.9),
        "norm_bias": gaussian(key_of[3], (CHANNELS,), 0.5, 3.0, (), jnp.float32),
        "conv_weight": gaussian(key_of[4], (CHANNELS, 27, CHANNELS), (27 * CHANNELS) ** -0.5, 0.0625, ((0, 16),)),
        "conv_bias": gaussian(key_of[5], (CHANNELS,), 0.5, 3.0, (), jnp.float32),
        "up_weight": gaussian(key_of[6], (OUT_CHANNELS, 9, CHANNELS), (9 * CHANNELS) ** -0.5, 0.109375, ((0, 16),)),
        "up_bias": gaussian(key_of[7], (OUT_CHANNELS,), 0.5, 3.0, (), jnp.float32),
    }


epsilon = 1e-06

def reference(features, skip, norm_gain, norm_bias, conv_weight, conv_bias, up_weight, up_bias):
    frames, row_count, col_count, chan_count = features.shape
    group_width = chan_count // GROUPS
    values = features.astype(jnp.float32).reshape(frames, row_count, col_count, GROUPS, group_width)
    group_mean = lax.optimization_barrier(jnp.mean(values, axis=(1, 2, 4), keepdims=True))
    centered = values - group_mean
    group_spread = lax.optimization_barrier(jnp.mean(centered * centered, axis=(1, 2, 4), keepdims=True))
    normed = (centered * lax.rsqrt(group_spread + epsilon)).reshape(frames, row_count, col_count, chan_count)
    activated = jax.nn.silu(normed * norm_gain + norm_bias).astype(jnp.bfloat16)
    padded = jnp.pad(activated, ((2, 0), (1, 1), (1, 1), (0, 0)))

    def one_frame(frame_index):
        frame_start = frame_index.astype(jnp.int32)
        zero_start = jnp.zeros((), jnp.int32)
        window = lax.dynamic_slice(padded, (frame_start, zero_start, zero_start, zero_start), (3, row_count + 2, col_count + 2, chan_count))
        summed_terms = jnp.zeros((row_count * col_count, conv_weight.shape[0]), jnp.float32)
        for kernel_tap in range(27):
            time_step, row_step, col_step = (kernel_tap // 9, kernel_tap // 3 % 3, kernel_tap % 3)
            window_slice = window[time_step, row_step:row_step + row_count, col_step:col_step + col_count].reshape(-1, chan_count)
            summed_terms = summed_terms + jnp.dot(window_slice, conv_weight[:, kernel_tap, :].T, preferred_element_type=jnp.float32)
        skip_frame = lax.dynamic_index_in_dim(skip, frame_start, 0, keepdims=False)
        summed = (skip_frame.astype(jnp.float32) + summed_terms.reshape(row_count, col_count, -1) + conv_bias).astype(jnp.bfloat16)
        lifted = jnp.repeat(jnp.repeat(summed, 2, axis=0), 2, axis=1)
        lifted = jnp.pad(lifted, ((1, 1), (1, 1), (0, 0)))
        result = jnp.zeros((4 * row_count * col_count, up_weight.shape[0]), jnp.float32)
        for kernel_tap in range(9):
            row_step, col_step = (kernel_tap // 3, kernel_tap % 3)
            window_slice = lifted[row_step:row_step + 2 * row_count, col_step:col_step + 2 * col_count].reshape(-1, chan_count)
            result = result + jnp.dot(window_slice, up_weight[:, kernel_tap, :].T, preferred_element_type=jnp.float32)
        return (result + up_bias).reshape(2 * row_count, 2 * col_count, -1).astype(jnp.bfloat16)
    return lax.map(one_frame, jnp.arange(frames, dtype=jnp.int32))
```

```python
import jax
import jax.numpy as jnp
from jax import lax
from jax.experimental import pallas as pl
from jax.experimental.pallas import tpu as pltpu
from jax.sharding import Mesh
from jax.sharding import PartitionSpec as P

GROUPS = 32
EPSILON = 1e-06
TILE = ("x", "y", "c")


def strip_shift(array, sizes, by):
    count = sizes["x"] * sizes["y"] * sizes["c"]
    return lax.ppermute(array, TILE, [(i, i + by) for i in range(count) if 0 <= i + by < count])


def sibling(array, sizes):
    count = sizes["x"] * sizes["y"] * sizes["c"]
    return lax.ppermute(array, TILE, [(i, i ^ 1) for i in range(count)])


def local_stats(frames6):
    frames, rows, cols, chans = frames6.shape
    width = chans // GROUPS
    values = frames6.astype(jnp.float32)
    chan_mean = jnp.mean(values, axis=(1, 2))
    centered = values - chan_mean[:, None, None, :]
    chan_m2 = jnp.sum(centered * centered, axis=(1, 2))
    chan_mean = chan_mean.reshape(frames, GROUPS, width)
    mean = jnp.mean(chan_mean, axis=2)
    apart = chan_mean - mean[:, :, None]
    m2 = jnp.sum(chan_m2.reshape(frames, GROUPS, width) + rows * cols * apart * apart, axis=2)
    return jnp.stack([mean, m2])


def whole_stats(local, sizes, members):
    count = sizes["x"] * sizes["y"] * sizes["c"]
    spread_out = jnp.broadcast_to(local[None], (count,) + local.shape)
    everyone = lax.all_to_all(spread_out, TILE, 0, 0, tiled=True)
    mean = jnp.mean(everyone[:, 0], axis=0)
    apart = everyone[:, 0] - mean
    m2 = jnp.sum(everyone[:, 1] + members * apart * apart, axis=0)
    return mean, lax.rsqrt(m2 / (members * count) + EPSILON)


def conv_kernel(core_ref, act_ref, weight_ref, out_ref):
    step = pl.program_id(0)
    core = core_ref[0]
    cols = out_ref.shape[0] // act_ref.shape[2]

    @pl.when(step == 0)
    def _():
        out_ref[...] = jnp.zeros_like(out_ref)

    for inner in range(2):
        tap = core * 13 + step * 2 + inner

        def add():
            window = act_ref[tap // 3, pl.ds(tap % 3, cols)].reshape(out_ref.shape[0], -1)
            out_ref[...] += lax.dot_general(
                window, weight_ref[inner], (((1,), (1,)), ((), ())), preferred_element_type=jnp.float32
            )

        if inner == 0:
            pl.when(jnp.logical_or(core == 0, step > 0))(add)
        else:
            add()


def conv_partial(core, act9, weight):
    taps, outs, chans = weight.shape
    positions = (act9.shape[1] - 2) * act9.shape[2]
    return pl.pallas_call(
        conv_kernel,
        grid=(taps // 2,),
        out_shape=jax.ShapeDtypeStruct((positions, outs), jnp.float32),
        in_specs=[
            pl.BlockSpec(memory_space=pltpu.SMEM),
            pl.BlockSpec(act9.shape, lambda i: (0, 0, 0, 0)),
            pl.BlockSpec((2, outs, chans), lambda i: (i, 0, 0)),
        ],
        out_specs=pl.BlockSpec((positions, outs), lambda i: (0, 0)),
        compiler_params=pltpu.CompilerParams(vmem_limit_bytes=32 * 1024 * 1024),
        cost_estimate=pl.CostEstimate(
            flops=2 * positions * outs * chans * taps, bytes_accessed=weight.size * 2, transcendentals=0
        ),
    )(core.reshape(1), act9, weight)


def per_device(sizes, features, skip, norm_gain, norm_bias, conv_weight, conv_bias, up_weight, up_bias):
    frames, rows, cols, chans = features.shape
    strips = sizes["x"] * sizes["y"] * sizes["c"]
    core = lax.axis_index("c")
    pair = lax.axis_index("x") * sizes["y"] + lax.axis_index("y")
    time = lax.axis_index("tm")
    shard = conv_weight.shape[0]

    by_tap = conv_weight.transpose(1, 0, 2)
    share = shard // sizes["y"]
    mine = lax.dynamic_slice(by_tap, (core * 13, lax.axis_index("y") * share, 0), (14, share, chans))
    half_kernel = lax.all_gather(mine, ("tm", "y"), axis=1, tiled=True)

    up_shard, up_taps, _ = up_weight.shape
    half = up_shard // 2
    up_mine = lax.dynamic_slice_in_dim(up_weight, core * half, half, axis=0)
    up_half = lax.all_to_all(
        jnp.broadcast_to(up_mine[None], (sizes["tm"],) + up_mine.shape), "tm", 0, 0, tiled=True
    )
    up_other = sibling(up_half, sizes)
    first = core == 0
    upper = jnp.stack([jnp.where(first, up_half, up_other), jnp.where(first, up_other, up_half)], axis=1)
    upper = upper.reshape(sizes["tm"] * up_shard, up_taps, chans)

    earlier = lax.ppermute(features[frames - 2 :], "tm", [(i, i + 1) for i in range(sizes["tm"] - 1)])
    frames6 = jnp.concatenate([earlier, features], axis=0)
    mean, scale = whole_stats(local_stats(frames6), sizes, float(rows * cols * (chans // GROUPS)))
    parcel = jnp.concatenate([frames6, skip], axis=0)
    other = sibling(parcel, sizes)
    both = jnp.concatenate([jnp.where(first, parcel, other), jnp.where(first, other, parcel)], axis=2)
    left = strip_shift(both[:, :, 2 * cols - 2 :], sizes, 2)
    right = strip_shift(both[:, :, :2], sizes, -2)
    wide = jnp.concatenate([left, both, right], axis=2)

    width = chans // GROUPS
    mean = jnp.repeat(mean, width, axis=1)[:, None, None, :]
    scale = jnp.repeat(scale, width, axis=1)[:, None, None, :]
    normed = (wide[: frames + 2].astype(jnp.float32) - mean) * scale
    activated = jax.nn.silu(normed * norm_gain + norm_bias)
    column = pair * 2 * cols - 2 + jnp.arange(2 * cols + 4)
    inside = jnp.logical_and(column >= 0, column < strips * cols)
    known = jnp.logical_or(time > 0, jnp.arange(frames + 2) >= 2)
    keep = jnp.logical_and(known[:, None, None, None], inside[None, None, :, None])
    activated = jnp.where(keep, activated, 0.0).astype(jnp.bfloat16)

    turned = jnp.pad(activated, ((0, 0), (1, 1), (0, 0), (0, 0))).transpose(2, 1, 0, 3)
    act9 = jnp.stack(
        [
            turned[:, dy : dy + rows, dt : dt + frames].reshape(2 * cols + 4, rows * frames, chans)
            for dt in range(3)
            for dy in range(3)
        ]
    )
    partial = conv_partial(core, act9, half_kernel).reshape(2 * cols + 2, rows * frames, chans)
    own = lax.dynamic_slice_in_dim(partial, core * cols, cols + 2, axis=0)
    sent = lax.dynamic_slice_in_dim(partial, (1 - core) * cols, cols + 2, axis=0)
    convolved = own + sibling(sent, sizes)

    skip10 = lax.dynamic_slice_in_dim(wide[frames + 2 :], 1 + core * cols, cols + 2, axis=2)
    summed = skip10.transpose(2, 1, 0, 3).reshape(cols + 2, rows * frames, chans).astype(jnp.float32)
    summed = summed + convolved + conv_bias
    inside10 = lax.dynamic_slice_in_dim(inside, 1 + core * cols, cols + 2)
    summed = jnp.where(inside10[:, None, None], summed, 0.0).astype(jnp.bfloat16)

    outs = upper.shape[0]
    taps = lax.dot_general(
        summed.reshape(-1, chans),
        upper.transpose(1, 0, 2).reshape(up_taps * outs, chans),
        (((1,), (1,)), ((), ())),
        preferred_element_type=jnp.float32,
    ).reshape(cols + 2, rows, frames, 3, 3, outs)
    taps = jnp.pad(taps, ((0, 0), (1, 1), (0, 0), (0, 0), (0, 0), (0, 0)))
    phases = []
    for low in range(2):
        line = 0.0
        for dy in range(3):
            at = 1 + (low + dy - 1) // 2
            line = line + taps[:, at : at + rows, :, dy]
        for side in range(2):
            total = 0.0
            for dx in range(3):
                at = 1 + (side + dx - 1) // 2
                total = total + line[at : at + cols, :, :, dx]
            phases.append((total + up_bias).astype(jnp.bfloat16))
    fine = jnp.stack(phases).reshape(2, 2, cols, rows, frames, outs)
    return fine.transpose(4, 3, 0, 2, 1, 5).reshape(frames, 2 * rows, 2 * cols, outs)


def solution(mesh):
    strips = mesh.shape["tile"]
    side = 1
    while side * side * 2 < strips:
        side *= 2
    sizes = {"tm": mesh.shape["tm"], "x": strips // (2 * side), "y": side, "c": 2}
    fine_mesh = Mesh(mesh.devices.reshape(tuple(sizes.values())), tuple(sizes))

    def body(*arrays):
        return per_device(sizes, *arrays)

    return jax.shard_map(
        body,
        mesh=fine_mesh,
        in_specs=(
            P("tm", None, TILE, None),
            P("tm", None, TILE, None),
            P(),
            P(),
            P("tm", None, None),
            P(),
            P("tm", None, None),
            P(),
        ),
        out_specs=P("tm", None, TILE, None),
        check_vma=False,
    )
```

```python
import jax
import jax.numpy as jnp
from jax import lax
from jax.experimental import pallas as pl
from jax.experimental.pallas import tpu as pltpu
from jax.sharding import Mesh
from jax.sharding import PartitionSpec as P

GROUPS = 32
EPSILON = 1e-06
TIME = ("m", "p")
TILE = ("x", "y1", "y0", "c")
QUAD = ("y0", "c")
TEAM = ("p", "y0", "c")
TAPS = 7
PADDED = 48
NT = (((1,), (1,)), ((), ()))


def swap(array, axis):
    return lax.ppermute(array, axis, [(0, 1), (1, 0)])


def strip_shift(array, count, by):
    return lax.ppermute(array, TILE, [(i, i + by) for i in range(count) if 0 <= i + by < count])


def handed_out(array, axes, members):
    return lax.all_to_all(jnp.broadcast_to(array[None], (members,) + array.shape), axes, 0, 0, tiled=True)


def local_stats(values):
    frames, rows, cols, chans = values.shape
    width = chans // GROUPS
    values = values.astype(jnp.float32)
    chan_mean = jnp.mean(values, axis=(1, 2))
    centered = values - chan_mean[:, None, None, :]
    chan_m2 = jnp.sum(centered * centered, axis=(1, 2))
    chan_mean = chan_mean.reshape(frames, GROUPS, width)
    mean = jnp.mean(chan_mean, axis=2)
    apart = chan_mean - mean[:, :, None]
    m2 = jnp.sum(chan_m2.reshape(frames, GROUPS, width) + rows * cols * apart * apart, axis=2)
    return jnp.concatenate([mean, m2], axis=1)


def whole_stats(everyone, members):
    means, m2s = everyone[:, :, :GROUPS], everyone[:, :, GROUPS:]
    mean = jnp.mean(means, axis=0)
    apart = means - mean
    m2 = jnp.sum(m2s + members * apart * apart, axis=0)
    return mean, lax.rsqrt(m2 / (members * everyone.shape[0]) + EPSILON)


def act_kernel(place_ref, wide_ref, mean_ref, scale_ref, gain_ref, bias_ref, out_ref, *, columns):
    frame = pl.program_id(0)
    rows, padded, chans = wide_ref.shape[1:]
    column = place_ref[0] + lax.broadcasted_iota(jnp.int32, (padded, chans), 0)
    keep = jnp.logical_and(column >= 0, column < columns)
    keep = jnp.logical_and(keep, jnp.logical_or(place_ref[1] > 0, frame >= 2))
    nothing = jnp.zeros((padded, chans), out_ref.dtype)
    for dx in range(3):
        out_ref[dx, 0, 0] = nothing
        out_ref[dx, 0, rows + 1] = nothing
    for row in range(rows):
        normed = (wide_ref[0, row].astype(jnp.float32) - mean_ref[0]) * scale_ref[0]
        value = normed * gain_ref[...] + bias_ref[...]
        value = jnp.where(keep, value / (1.0 + jnp.exp(-value)), 0.0)
        for dx in range(3):
            moved = value if dx == 0 else pltpu.roll(value, padded - dx, 0)
            out_ref[dx, 0, row + 1] = moved.astype(out_ref.dtype)


def activate(place, wide, mean, scale, gain, bias, columns):
    frames, rows, padded, chans = wide.shape
    line = pl.BlockSpec((1, 1, chans), lambda t: (t, 0, 0))
    vector = pl.BlockSpec((1, chans), lambda t: (0, 0))

    def kernel(*refs):
        act_kernel(*refs, columns=columns)

    return pl.pallas_call(
        kernel,
        grid=(frames,),
        out_shape=jax.ShapeDtypeStruct((3, frames, rows + 2, padded, chans), jnp.bfloat16),
        in_specs=[
            pl.BlockSpec(memory_space=pltpu.SMEM),
            pl.BlockSpec((1, rows, padded, chans), lambda t: (t, 0, 0, 0)),
            line,
            line,
            vector,
            vector,
        ],
        out_specs=pl.BlockSpec((3, 1, rows + 2, padded, chans), lambda t: (0, t, 0, 0, 0)),
        cost_estimate=pl.CostEstimate(flops=20 * wide.size, bytes_accessed=12 * wide.size, transcendentals=wide.size),
    )(place, wide, mean[:, None], scale[:, None], gain[None], bias[None])


def conv_kernel(place_ref, act_ref, weight_ref, out_ref, total_ref):
    step = pl.program_id(0)
    frames, rows, padded, outs = total_ref.shape

    @pl.when(step == 0)
    def _():
        total_ref[...] = jnp.zeros_like(total_ref)

    tap = place_ref[0] + step

    @pl.when(jnp.logical_or(step > 0, place_ref[1] == 0))
    def _():
        for frame in range(frames):
            window = act_ref[tap % 3, tap // 9 + frame, pl.ds(tap // 3 % 3, rows)]
            part = lax.dot_general(
                window.reshape(rows * padded, -1), weight_ref[0], NT, preferred_element_type=jnp.float32
            )
            total_ref[frame] += part.reshape(rows, padded, outs)

    @pl.when(step == pl.num_programs(0) - 1)
    def _():
        for member in range(out_ref.shape[0]):
            plane, strip = member // 4, member % 4
            span = out_ref.shape[1]
            part = total_ref[plane * span : (plane + 1) * span, :, strip * 8 : strip * 8 + 16]
            out_ref[member] = part.astype(out_ref.dtype)


def conv_partial(place, act, weight):
    taps, outs, chans = weight.shape
    _, frames, rows, padded, _ = act.shape
    frames, rows = frames - 2, rows - 2
    return pl.pallas_call(
        conv_kernel,
        grid=(taps,),
        out_shape=jax.ShapeDtypeStruct((8, frames // 2, rows, 16, outs), jnp.bfloat16),
        in_specs=[
            pl.BlockSpec(memory_space=pltpu.SMEM),
            pl.BlockSpec(act.shape, lambda i: (0, 0, 0, 0, 0)),
            pl.BlockSpec((1, outs, chans), lambda i: (i, 0, 0)),
        ],
        out_specs=pl.BlockSpec((8, frames // 2, rows, 16, outs), lambda i: (0, 0, 0, 0, 0)),
        scratch_shapes=[pltpu.VMEM((frames, rows, padded, outs), jnp.float32)],
        compiler_params=pltpu.CompilerParams(vmem_limit_bytes=40 * 1024 * 1024),
        cost_estimate=pl.CostEstimate(
            flops=2 * frames * rows * padded * outs * chans * taps,
            bytes_accessed=2 * (weight.size + act.size),
            transcendentals=0,
        ),
    )(place, act, weight)


def tail_kernel(place_ref, parts_ref, skip_ref, bias_ref, upper_ref, up_bias_ref, out_ref, tap_ref, fine_ref, *, columns):
    frames, rows, padded, outs = tap_ref.shape[1:]
    half = parts_ref.shape[-1]
    column = place_ref[0] + lax.broadcasted_iota(jnp.int32, (frames, rows, padded, half), 2)
    keep = jnp.logical_and(column >= 0, column < columns)
    summed = []
    for parity in range(2):
        total = parts_ref[4 * parity].astype(jnp.float32)
        for quarter in range(1, 4):
            total = total + parts_ref[4 * parity + quarter].astype(jnp.float32)
        total = skip_ref[parity].astype(jnp.float32) + total + bias_ref[parity]
        total = jnp.where(keep, total, 0.0).astype(jnp.bfloat16)
        summed.append(total.reshape(frames * rows * padded, half))
    for tap in range(9):
        part = lax.dot_general(summed[0], upper_ref[0, tap], NT, preferred_element_type=jnp.float32)
        part = part + lax.dot_general(summed[1], upper_ref[1, tap], NT, preferred_element_type=jnp.float32)
        tap_ref[tap] = part.reshape(frames, rows, padded, outs)

    cols = padded // 2
    for frame in range(frames):
        for row in range(rows):
            for low in range(2):
                lines = []
                for dx in range(3):
                    line = 0.0
                    for dy in range(3):
                        at = row + (low + dy - 1) // 2
                        if 0 <= at < rows:
                            line = line + tap_ref[3 * dy + dx, frame, at]
                    lines.append(line)
                left = lines[0][0:cols] + (lines[1] + lines[2])[1 : 1 + cols]
                right = (lines[0] + lines[1])[1 : 1 + cols] + lines[2][2 : 2 + cols]
                for side, value in ((0, left), (1, right)):
                    value = value + up_bias_ref[...]
                    spare = jnp.zeros((cols, 256 - outs), jnp.float32)
                    fine_ref[0, pl.ds(side, cols, stride=2), :] = value[:, :128]
                    fine_ref[1, pl.ds(side, cols, stride=2), :] = jnp.concatenate([value[:, 128:], spare], axis=1)
                out_ref[frame, 2 * row + low, :, 0:128] = fine_ref[0].astype(out_ref.dtype)
                out_ref[frame, 2 * row + low, :, 128:outs] = fine_ref[1, :, : outs - 128].astype(out_ref.dtype)


def tail(place, parts, skip, bias, upper, up_bias, columns):
    _, frames, rows, padded, _ = parts.shape
    outs = upper.shape[2]

    def kernel(*refs):
        tail_kernel(*refs, columns=columns)

    vmem = pl.BlockSpec(memory_space=pltpu.VMEM)
    return pl.pallas_call(
        kernel,
        out_shape=jax.ShapeDtypeStruct((frames, 2 * rows, padded, outs), jnp.bfloat16),
        in_specs=[pl.BlockSpec(memory_space=pltpu.SMEM)] + [vmem] * 5,
        out_specs=vmem,
        scratch_shapes=[
            pltpu.VMEM((9, frames, rows, padded, outs), jnp.float32),
            pltpu.VMEM((2, padded, 128), jnp.float32),
        ],
        compiler_params=pltpu.CompilerParams(vmem_limit_bytes=40 * 1024 * 1024),
        cost_estimate=pl.CostEstimate(
            flops=2 * frames * rows * padded * upper.size, bytes_accessed=2 * upper.size, transcendentals=0
        ),
    )(place, parts, skip, bias, upper, up_bias)


def per_device(sizes, features, skip, norm_gain, norm_bias, conv_weight, conv_bias, up_weight, up_bias):
    frames, rows, cols, chans = features.shape
    strips = sizes["x"] * sizes["y1"] * 4
    columns = strips * cols
    planes = sizes["m"] * 2
    quarter = 2 * lax.axis_index("y0") + lax.axis_index("c")
    quad = lax.axis_index("x") * sizes["y1"] + lax.axis_index("y1")
    strip = 4 * quad + quarter
    pair = lax.axis_index("m")

    first_tap = jnp.minimum(quarter * TAPS, 27 - TAPS)
    mine = lax.dynamic_slice_in_dim(conv_weight, first_tap, TAPS, axis=1)
    kernel = lax.all_gather(mine, "m", axis=0, tiled=True).transpose(1, 0, 2)

    other = swap(features, "p")
    first = lax.axis_index("p") == 0
    eight = jnp.concatenate([jnp.where(first, features, other), jnp.where(first, other, features)], axis=0)
    back = lax.ppermute(eight[2 * frames - 2 :], "m", [(i, i + 1) for i in range(sizes["m"] - 1)])
    ten = jnp.concatenate([back, eight], axis=0)
    up_shard, up_taps, _ = up_weight.shape
    share = up_shard // 4
    up_mine = lax.dynamic_slice_in_dim(up_weight, quarter * share, share, axis=0)
    up_mine, ten = lax.optimization_barrier((up_mine, ten))
    up_mine = handed_out(up_mine, TIME, planes)
    everyone = handed_out(local_stats(ten), TILE, strips)

    other = swap(ten, "c")
    first = lax.axis_index("c") == 0
    both = jnp.concatenate([jnp.where(first, ten, other), jnp.where(first, other, ten)], axis=2)
    up_mine, both = lax.optimization_barrier((up_mine, both))
    up_all = handed_out(up_mine, QUAD, 4)
    other = swap(both, "y0")
    first = lax.axis_index("y0") == 0
    four = jnp.concatenate([jnp.where(first, both, other), jnp.where(first, other, both)], axis=2)
    skip, four = lax.optimization_barrier((skip, four))
    left = strip_shift(four[:, :, 4 * cols - 2 :], strips, 4)
    right = strip_shift(four[:, :, :2], strips, -4)
    rest = jnp.zeros((2 * frames + 2, rows, PADDED - 4 * cols - 4, chans), features.dtype)
    wide = jnp.concatenate([left, four, right, rest], axis=2)

    upper = up_all.transpose(3, 1, 0, 2, 4).reshape(up_taps * planes * up_shard, chans)

    shard = conv_weight.shape[0]
    place = jnp.arange(chans).reshape(sizes["m"], 2, shard).transpose(1, 0, 2).reshape(2, chans // 2)
    pick = (place[:, None, :] == jnp.arange(chans)[None, :, None]).astype(jnp.bfloat16)
    upper = lax.dot_general(upper, pick, (((1,), (1,)), ((), ())), preferred_element_type=jnp.float32)
    upper = upper.astype(jnp.bfloat16).reshape(up_taps, planes * up_shard, 2, chans // 2).transpose(2, 0, 1, 3)
    skip_left = strip_shift(skip[:, :, cols - 1 :], strips, 1)
    skip_right = strip_shift(skip[:, :, :1], strips, -1)
    skip_rest = jnp.zeros((frames, rows, cols - 2, chans), skip.dtype)
    skip16 = jnp.concatenate([skip_left, skip, skip_right, skip_rest], axis=2)
    skip16 = [
        jnp.dot(skip16.reshape(-1, chans), pick[parity], preferred_element_type=jnp.float32)
        .astype(jnp.bfloat16)
        .reshape(frames, rows, 2 * cols, chans // 2)
        for parity in range(2)
    ]
    bias = conv_bias.reshape(sizes["m"], 2, shard).transpose(1, 0, 2).reshape(2, 1, 1, 1, chans // 2)

    width = chans // GROUPS
    mean, scale = whole_stats(everyone, float(rows * cols * width))
    mean = jnp.repeat(mean, width, axis=1)
    scale = jnp.repeat(scale, width, axis=1)
    act = activate(
        jnp.stack([quad * 4 * cols - 2, pair]), wide, mean, scale, norm_gain, norm_bias, columns
    )
    parts = conv_partial(jnp.stack([first_tap, (quarter == 3).astype(jnp.int32)]), act, kernel)
    parts = lax.all_to_all(parts, TEAM, 0, 0, tiled=True)
    return tail(
        (strip * cols - 1).reshape(1), parts, jnp.stack(skip16), bias, upper, up_bias[None], columns
    )


def solution(mesh):
    strips = mesh.shape["tile"]
    side = 2
    while side * side * 2 < strips:
        side *= 2
    sizes = {"m": mesh.shape["tm"] // 2, "p": 2, "x": strips // (2 * side), "y1": side // 2, "y0": 2, "c": 2}
    fine_mesh = Mesh(mesh.devices.reshape(tuple(sizes.values())), tuple(sizes))

    def body(*arrays):
        return per_device(sizes, *arrays)

    return jax.shard_map(
        body,
        mesh=fine_mesh,
        in_specs=(
            P(TIME, None, TILE, None),
            P(TIME, None, TILE, None),
            P(),
            P(),
            P(TIME, None, None),
            P(),
            P(TIME, None, None),
            P(),
        ),
        out_specs=P(TIME, None, TILE, None),
        check_vma=False,
    )
```

```python
import jax
import jax.numpy as jnp
from jax import lax
from jax.experimental import pallas as pl
from jax.experimental.pallas import tpu as pltpu
from jax.sharding import Mesh
from jax.sharding import PartitionSpec as P

GROUPS = 32
EPSILON = 1e-06
TIME = ("m", "p")
TILE = ("x", "y1", "y0", "c")
QUAD = ("y0", "c")
TEAM = ("p", "y0", "c")
TAPS = 7
PADDED = 48
NT = (((1,), (1,)), ((), ()))


def swap(array, axis):
    return lax.ppermute(array, axis, [(0, 1), (1, 0)])


def strip_shift(array, count, by):
    return lax.ppermute(array, TILE, [(i, i + by) for i in range(count) if 0 <= i + by < count])


def handed_out(array, axes, members):
    return lax.all_to_all(jnp.broadcast_to(array[None], (members,) + array.shape), axes, 0, 0, tiled=True)


def local_stats(values):
    frames, rows, cols, chans = values.shape
    width = chans // GROUPS
    values = values.astype(jnp.float32)
    chan_mean = jnp.mean(values, axis=(1, 2))
    centered = values - chan_mean[:, None, None, :]
    chan_m2 = jnp.sum(centered * centered, axis=(1, 2))
    chan_mean = chan_mean.reshape(frames, GROUPS, width)
    mean = jnp.mean(chan_mean, axis=2)
    apart = chan_mean - mean[:, :, None]
    m2 = jnp.sum(chan_m2.reshape(frames, GROUPS, width) + rows * cols * apart * apart, axis=2)
    return jnp.concatenate([mean, m2], axis=1)


def whole_stats(everyone, members):
    means, m2s = everyone[:, :, :GROUPS], everyone[:, :, GROUPS:]
    mean = jnp.mean(means, axis=0)
    apart = means - mean
    m2 = jnp.sum(m2s + members * apart * apart, axis=0)
    return mean, lax.rsqrt(m2 / (members * everyone.shape[0]) + EPSILON)


def act_kernel(
    place_ref, own_ref, by_y_ref, by_c_ref, by_yc_ref, left_ref, right_ref, mean_ref, scale_ref, gain_ref, bias_ref,
    out_ref, slab_ref, *, columns,
):
    frames, rows, cols, chans = own_ref.shape
    padded = slab_ref.shape[0]
    first, pair, quarter = place_ref[0], place_ref[1], place_ref[2]
    column = first - 6 + lax.broadcasted_iota(jnp.int32, (padded, chans), 0)
    inside = jnp.logical_and(column >= 0, column < columns)
    slab_ref[...] = jnp.zeros_like(slab_ref)
    nothing = jnp.zeros((padded, chans), out_ref.dtype)

    def one_frame(frame, carry):
        keep = jnp.logical_and(inside, jnp.logical_or(pair > 0, frame >= 2))
        gain = scale_ref[frame] * gain_ref[...]
        for dx in range(3):
            out_ref[dx, frame, 0] = nothing
            out_ref[dx, frame, rows + 1] = nothing
        for row in range(rows):
            for flip, ref in enumerate((own_ref, by_c_ref, by_y_ref, by_yc_ref)):
                at = pl.multiple_of(8 + cols * jnp.bitwise_xor(quarter, flip), 8)
                slab_ref[pl.ds(at, cols), :] = ref[frame, row].astype(jnp.float32)
            slab_ref[6:8, :] = left_ref[frame, row].astype(jnp.float32)
            slab_ref[8 + 4 * cols : 10 + 4 * cols, :] = right_ref[frame, row].astype(jnp.float32)
            value = (slab_ref[...] - mean_ref[frame]) * gain + bias_ref[...]
            value = 0.5 * value
            value = jnp.where(keep, value + value * jnp.tanh(value), 0.0)
            for dx in range(3):
                out_ref[dx, frame, row + 1] = pltpu.roll(value, padded - 6 - dx, 0).astype(out_ref.dtype)
        return carry

    lax.fori_loop(0, frames, one_frame, 0)


def activate(place, strips, left, right, mean, scale, gain, bias, columns):
    frames, rows, cols, chans = strips[0].shape

    def kernel(*refs):
        act_kernel(*refs, columns=columns)

    vmem = pl.BlockSpec(memory_space=pltpu.VMEM)
    return pl.pallas_call(
        kernel,
        out_shape=jax.ShapeDtypeStruct((3, frames, rows + 2, PADDED, chans), jnp.bfloat16),
        in_specs=[pl.BlockSpec(memory_space=pltpu.SMEM)] + [vmem] * 10,
        out_specs=vmem,
        scratch_shapes=[pltpu.VMEM((PADDED, chans), jnp.float32)],
        compiler_params=pltpu.CompilerParams(vmem_limit_bytes=40 * 1024 * 1024),
        cost_estimate=pl.CostEstimate(
            flops=100 * strips[0].size, bytes_accessed=60 * strips[0].size, transcendentals=6 * strips[0].size
        ),
    )(place, *strips, left, right, mean[:, None], scale[:, None], gain[None], bias[None])


def conv_kernel(place_ref, act_ref, weight_ref, out_ref, total_ref, held_ref, arrived):
    frames, rows, padded, outs = total_ref.shape
    taps = held_ref.shape[0]
    copies = [pltpu.make_async_copy(weight_ref.at[i], held_ref.at[i], arrived.at[i]) for i in range(taps)]
    for copy in copies:
        copy.start()
    doubled = (place_ref[1] > 0).astype(jnp.float32)
    for i in range(taps):
        copies[i].wait()
        tap = place_ref[0] + i
        window = act_ref[tap % 3, pl.ds(tap // 9, frames), pl.ds(tap // 3 % 3, rows)]
        part = lax.dot_general(
            window.reshape(frames * rows * padded, -1), held_ref[i], NT, preferred_element_type=jnp.float32
        ).reshape(total_ref.shape)
        if i == 0:
            total_ref[...] = part * (1.0 - doubled)
        else:
            total_ref[...] += part
    span = out_ref.shape[1]
    for member in range(out_ref.shape[0]):
        plane, strip = member // 4, member % 4
        part = total_ref[plane * span : (plane + 1) * span, :, strip * 8 : strip * 8 + 16]
        out_ref[member] = part.astype(out_ref.dtype)


def conv_partial(place, act, weight):
    slots, outs, chans = weight.shape
    _, frames, rows, padded, _ = act.shape
    frames, rows = frames - 2, rows - 2
    vmem = pl.BlockSpec(memory_space=pltpu.VMEM)
    return pl.pallas_call(
        conv_kernel,
        out_shape=jax.ShapeDtypeStruct((8, frames // 2, rows, 16, outs), jnp.bfloat16),
        in_specs=[pl.BlockSpec(memory_space=pltpu.SMEM), vmem, pl.BlockSpec(memory_space=pl.ANY)],
        out_specs=vmem,
        scratch_shapes=[
            pltpu.VMEM((frames, rows, padded, outs), jnp.float32),
            pltpu.VMEM((TAPS, outs, chans), jnp.bfloat16),
            pltpu.SemaphoreType.DMA((TAPS,)),
        ],
        compiler_params=pltpu.CompilerParams(vmem_limit_bytes=40 * 1024 * 1024),
        cost_estimate=pl.CostEstimate(
            flops=2 * frames * rows * padded * outs * chans * TAPS,
            bytes_accessed=2 * (TAPS * outs * chans + act.size),
            transcendentals=0,
        ),
    )(place, act, weight)


def tail_kernel(
    place_ref, parts_ref, skip_ref, bias_ref, pick_ref, upper_ref, up_bias_ref, out_ref, tap_ref, fine_ref, *, columns
):
    frames, rows, padded, outs = tap_ref.shape[1:]
    chans = skip_ref.shape[-1]
    flat = (frames * rows * padded, -1)
    column = place_ref[0] + lax.broadcasted_iota(jnp.int32, (frames, rows, padded, chans), 2)
    keep = jnp.logical_and(column >= 0, column < columns)
    summed = skip_ref[...].astype(jnp.float32).reshape(flat[0], chans) + bias_ref[...]
    for parity in range(2):
        total = parts_ref[4 * parity].astype(jnp.float32)
        for quarter in range(1, 4):
            total = total + parts_ref[4 * parity + quarter].astype(jnp.float32)
        total = total.reshape(flat)
        upper_half = total.astype(jnp.bfloat16)
        lower_half = (total - upper_half.astype(jnp.float32)).astype(jnp.bfloat16)
        for part in (lower_half, upper_half):
            summed = summed + jnp.dot(part, pick_ref[parity], preferred_element_type=jnp.float32)
    summed = jnp.where(keep.reshape(flat[0], chans), summed, 0.0).astype(jnp.bfloat16)
    for tap in range(9):
        part = lax.dot_general(summed, upper_ref[tap], NT, preferred_element_type=jnp.float32)
        tap_ref[tap] = part.reshape(frames, rows, padded, outs)

    cols = padded // 2
    for frame in range(frames):
        for row in range(rows):
            for low in range(2):
                lines = []
                for dx in range(3):
                    line = 0.0
                    for dy in range(3):
                        at = row + (low + dy - 1) // 2
                        if 0 <= at < rows:
                            line = line + tap_ref[3 * dy + dx, frame, at]
                    lines.append(line)
                left = lines[0][0:cols] + (lines[1] + lines[2])[1 : 1 + cols]
                right = (lines[0] + lines[1])[1 : 1 + cols] + lines[2][2 : 2 + cols]
                for side, value in ((0, left), (1, right)):
                    value = value + up_bias_ref[...]
                    spare = jnp.zeros((cols, 256 - outs), jnp.float32)
                    fine_ref[0, pl.ds(side, cols, stride=2), :] = value[:, :128]
                    fine_ref[1, pl.ds(side, cols, stride=2), :] = jnp.concatenate([value[:, 128:], spare], axis=1)
                out_ref[frame, 2 * row + low, :, 0:128] = fine_ref[0].astype(out_ref.dtype)
                out_ref[frame, 2 * row + low, :, 128:outs] = fine_ref[1, :, : outs - 128].astype(out_ref.dtype)


def tail(place, parts, skip, bias, pick, upper, up_bias, columns):
    _, frames, rows, padded, _ = parts.shape
    outs = upper.shape[1]

    def kernel(*refs):
        tail_kernel(*refs, columns=columns)

    vmem = pl.BlockSpec(memory_space=pltpu.VMEM)
    return pl.pallas_call(
        kernel,
        out_shape=jax.ShapeDtypeStruct((frames, 2 * rows, padded, outs), jnp.bfloat16),
        in_specs=[pl.BlockSpec(memory_space=pltpu.SMEM)] + [vmem] * 6,
        out_specs=vmem,
        scratch_shapes=[
            pltpu.VMEM((9, frames, rows, padded, outs), jnp.float32),
            pltpu.VMEM((2, padded, 128), jnp.float32),
        ],
        compiler_params=pltpu.CompilerParams(vmem_limit_bytes=40 * 1024 * 1024),
        cost_estimate=pl.CostEstimate(
            flops=2 * frames * rows * padded * upper.size, bytes_accessed=2 * upper.size, transcendentals=0
        ),
    )(place, parts, skip, bias, pick, upper, up_bias)


def per_device(sizes, features, skip, norm_gain, norm_bias, conv_weight, conv_bias, up_weight, up_bias):
    frames, rows, cols, chans = features.shape
    pairs = sizes["m"]
    strips = sizes["x"] * sizes["y1"] * 4
    columns = strips * cols
    core = lax.axis_index("c")
    quarter = 2 * lax.axis_index("y0") + core
    quad = lax.axis_index("x") * sizes["y1"] + lax.axis_index("y1")
    strip = 4 * quad + quarter
    even = lax.axis_index("p") == 0

    shard, up_shard = conv_weight.shape[0], up_weight.shape[0]
    first_tap = jnp.minimum(quarter * TAPS, 27 - TAPS)
    mine = lax.dynamic_slice_in_dim(conv_weight, first_tap, TAPS, axis=1)
    up_mine = lax.dynamic_slice_in_dim(up_weight, core * 3, 6, axis=1).reshape(up_shard, 3, 2, chans)
    up_mine = up_mine.transpose(2, 0, 1, 3).reshape(shard, 3, chans)
    mine = jnp.concatenate([mine, up_mine], axis=1)
    gathered = lax.all_gather(mine, "m", axis=0, tiled=True).transpose(1, 0, 2)

    other = swap(features, "p")
    eight = jnp.concatenate([jnp.where(even, features, other), jnp.where(even, other, features)], axis=0)
    back = lax.ppermute(eight[2 * frames - 2 :], "m", [(i, i + 1) for i in range(pairs - 1)])
    ten = jnp.concatenate([back, eight], axis=0)
    by_y = swap(ten, "y0")
    everyone = handed_out(local_stats(ten), TILE, strips)

    by_c = swap(jnp.stack([ten, by_y]), "c")
    held = (ten, by_c[0], by_y, by_c[1])
    head, tail_end = held[0][:, :, :2], held[0][:, :, cols - 2 :]
    for flip in range(1, 4):
        head = jnp.where(quarter == flip, held[flip][:, :, :2], head)
        tail_end = jnp.where(quarter == 3 - flip, held[flip][:, :, cols - 2 :], tail_end)
    skip, head, tail_end = lax.optimization_barrier((skip, head, tail_end))
    left = strip_shift(tail_end, strips, 4)
    right = strip_shift(head, strips, -4)
    skip_left = strip_shift(skip[:, :, cols - 1 :], strips, 1)
    skip_right = strip_shift(skip[:, :, :1], strips, -1)
    skip_rest = jnp.zeros((frames, rows, cols - 2, chans), skip.dtype)
    skip16 = jnp.concatenate([skip_left, skip, skip_right, skip_rest], axis=2)

    width = chans // GROUPS
    mean, scale = whole_stats(everyone, float(rows * cols * width))
    mean = jnp.repeat(mean, width, axis=1)
    scale = jnp.repeat(scale, width, axis=1)
    place = jnp.stack([quad * 4 * cols - 2, lax.axis_index("m"), quarter])
    act = activate(
        place, (ten, by_y, by_c[0], by_c[1]), left, right, mean, scale, norm_gain, norm_bias, columns
    )

    gathered, act = lax.optimization_barrier((gathered, act))
    up_own = gathered[TAPS:]
    other = swap(up_own, "p")
    up_pair = jnp.stack([jnp.where(even, up_own, other), jnp.where(even, other, up_own)])
    parts = conv_partial(jnp.stack([first_tap, (quarter == 3).astype(jnp.int32)]), act, gathered)
    other = swap(up_pair, "c")
    upper = [
        jnp.where(core == which, up_pair, other)
        .reshape(2, 3, pairs, 2, up_shard, chans)
        .transpose(1, 3, 2, 0, 4, 5)
        .reshape(6, 2 * pairs * up_shard, chans)
        for which in range(2)
    ]
    upper = jnp.concatenate([upper[0][:5], upper[1][2:]], axis=0)

    channel = jnp.arange(chans).reshape(pairs, 2, shard).transpose(1, 0, 2).reshape(2, chans // 2)
    pick = (channel[:, :, None] == jnp.arange(chans)[None, None, :]).astype(jnp.bfloat16)
    parts = lax.all_to_all(parts, TEAM, 0, 0, tiled=True)
    return tail(
        (strip * cols - 1).reshape(1), parts, skip16, conv_bias[None], pick, upper, up_bias[None], columns
    )


def solution(mesh):
    strips = mesh.shape["tile"]
    side = 2
    while side * side * 2 < strips:
        side *= 2
    sizes = {"m": mesh.shape["tm"] // 2, "p": 2, "x": strips // (2 * side), "y1": side // 2, "y0": 2, "c": 2}
    fine_mesh = Mesh(mesh.devices.reshape(tuple(sizes.values())), tuple(sizes))

    def body(*arrays):
        return per_device(sizes, *arrays)

    return jax.shard_map(
        body,
        mesh=fine_mesh,
        in_specs=(
            P(TIME, None, TILE, None),
            P(TIME, None, TILE, None),
            P(),
            P(),
            P(TIME, None, None),
            P(),
            P(TIME, None, None),
            P(),
        ),
        out_specs=P(TIME, None, TILE, None),
        check_vma=False,
    )
```

```python
import jax
import jax.numpy as jnp
from jax import lax
from jax.experimental import pallas as pl
from jax.experimental.pallas import tpu as pltpu
from jax.sharding import Mesh
from jax.sharding import PartitionSpec as P

GROUPS = 32
EPSILON = 1e-06
TIME = ("m", "p")
TILE = ("x", "y1", "y0", "c")
TEAM = ("p", "y0", "c")
TAPS = 7
PADDED = 48
NT = (((1,), (1,)), ((), ()))


def swap(array, axis):
    return lax.ppermute(array, axis, [(0, 1), (1, 0)])


def strip_shift(array, count, by):
    return lax.ppermute(array, TILE, [(i, i + by) for i in range(count) if 0 <= i + by < count])


def handed_out(array, axes, members):
    return lax.all_to_all(jnp.broadcast_to(array[None], (members,) + array.shape), axes, 0, 0, tiled=True)


def local_stats(values):
    frames, rows, cols, chans = values.shape
    width = chans // GROUPS
    values = values.astype(jnp.float32)
    chan_mean = jnp.mean(values, axis=(1, 2))
    centered = values - chan_mean[:, None, None, :]
    chan_m2 = jnp.sum(centered * centered, axis=(1, 2))
    chan_mean = chan_mean.reshape(frames, GROUPS, width)
    mean = jnp.mean(chan_mean, axis=2)
    apart = chan_mean - mean[:, :, None]
    m2 = jnp.sum(chan_m2.reshape(frames, GROUPS, width) + rows * cols * apart * apart, axis=2)
    return jnp.concatenate([mean, m2], axis=1)


def whole_stats(everyone, members):
    means, m2s = everyone[:, :, :GROUPS], everyone[:, :, GROUPS:]
    mean = jnp.mean(means, axis=0)
    apart = means - mean
    m2 = jnp.sum(m2s + members * apart * apart, axis=0)
    return mean, lax.rsqrt(m2 / (members * everyone.shape[0]) + EPSILON)


def act_kernel(
    place_ref, own_ref, by_y_ref, by_c_ref, by_yc_ref, left_ref, right_ref, mean_ref, scale_ref, gain_ref, bias_ref,
    out_ref, slab_ref, *, columns,
):
    frames, rows, cols, chans = own_ref.shape
    padded = slab_ref.shape[0]
    first, pair, quarter = place_ref[0], place_ref[1], place_ref[2]
    column = first - 6 + lax.broadcasted_iota(jnp.int32, (padded, chans), 0)
    inside = jnp.logical_and(column >= 0, column < columns)
    slab_ref[...] = jnp.zeros_like(slab_ref)
    nothing = jnp.zeros((padded, chans), out_ref.dtype)

    def one_frame(frame, carry):
        keep = jnp.logical_and(inside, jnp.logical_or(pair > 0, frame >= 2))
        gain = scale_ref[frame] * gain_ref[...]
        for dx in range(3):
            out_ref[dx, frame, 0] = nothing
            out_ref[dx, frame, rows + 1] = nothing
        for row in range(rows):
            for flip, ref in enumerate((own_ref, by_c_ref, by_y_ref, by_yc_ref)):
                at = pl.multiple_of(8 + cols * jnp.bitwise_xor(quarter, flip), 8)
                slab_ref[pl.ds(at, cols), :] = ref[frame, row].astype(jnp.float32)
            slab_ref[6:8, :] = left_ref[frame, row].astype(jnp.float32)
            slab_ref[8 + 4 * cols : 10 + 4 * cols, :] = right_ref[frame, row].astype(jnp.float32)
            value = (slab_ref[...] - mean_ref[frame]) * gain + bias_ref[...]
            value = 0.5 * value
            value = jnp.where(keep, value + value * jnp.tanh(value), 0.0)
            for dx in range(3):
                out_ref[dx, frame, row + 1] = pltpu.roll(value, padded - 6 - dx, 0).astype(out_ref.dtype)
        return carry

    lax.fori_loop(0, frames, one_frame, 0)


def activate(place, strips, left, right, mean, scale, gain, bias, columns):
    frames, rows, cols, chans = strips[0].shape

    def kernel(*refs):
        act_kernel(*refs, columns=columns)

    vmem = pl.BlockSpec(memory_space=pltpu.VMEM)
    return pl.pallas_call(
        kernel,
        out_shape=jax.ShapeDtypeStruct((3, frames, rows + 2, PADDED, chans), jnp.bfloat16),
        in_specs=[pl.BlockSpec(memory_space=pltpu.SMEM)] + [vmem] * 10,
        out_specs=vmem,
        scratch_shapes=[pltpu.VMEM((PADDED, chans), jnp.float32)],
        compiler_params=pltpu.CompilerParams(vmem_limit_bytes=40 * 1024 * 1024),
        cost_estimate=pl.CostEstimate(
            flops=100 * strips[0].size, bytes_accessed=60 * strips[0].size, transcendentals=6 * strips[0].size
        ),
    )(place, *strips, left, right, mean[:, None], scale[:, None], gain[None], bias[None])


def conv_kernel(place_ref, act_ref, weight_ref, out_ref, held_ref, stage_ref, arrived):
    taps, outs, _ = held_ref.shape
    frames, rows, padded = act_ref.shape[1] - 2, act_ref.shape[2] - 2, act_ref.shape[3]
    members, span = out_ref.shape[0], frames // 2
    cols = out_ref.shape[1] // (span * rows)
    first, doubled = place_ref[0], place_ref[1]
    copies = [
        pltpu.make_async_copy(weight_ref.at[doubled + i], held_ref.at[i], arrived.at[i]) for i in range(taps)
    ]
    for copy in copies:
        copy.start()
    counted = 1.0 - doubled.astype(jnp.float32)
    for chunk in range(0, frames, 2):
        total = None
        for i in range(taps):
            if chunk == 0:
                copies[i].wait()
            tap = first + i
            window = act_ref[tap % 3, pl.ds(tap // 9 + chunk, 2), pl.ds(tap // 3 % 3, rows)]
            part = lax.dot_general(
                window.reshape(2 * rows * padded, -1), held_ref[i], NT, preferred_element_type=jnp.float32
            )
            total = part * counted if i == 0 else total + part
        total = total.reshape(2, rows, padded, outs)
        for step in range(2):
            plane, frame = (chunk + step) // span, (chunk + step) % span
            for row in range(rows):
                at = (frame * rows + row) * cols
                for strip in range(4):
                    stage_ref[4 * plane + strip, at : at + cols, :] = total[step, row, strip * 8 : strip * 8 + cols]
    for member in range(members):
        out_ref[member] = stage_ref[member].astype(out_ref.dtype)


def conv_partial(place, act, weight, cols):
    slots, outs, chans = weight.shape
    _, frames, rows, padded, _ = act.shape
    frames, rows = frames - 2, rows - 2
    block = (8, frames // 2 * rows * cols, outs)
    vmem = pl.BlockSpec(memory_space=pltpu.VMEM)
    return pl.pallas_call(
        conv_kernel,
        out_shape=jax.ShapeDtypeStruct(block, jnp.bfloat16),
        in_specs=[pl.BlockSpec(memory_space=pltpu.SMEM), vmem, pl.BlockSpec(memory_space=pltpu.HBM)],
        out_specs=vmem,
        scratch_shapes=[
            pltpu.VMEM((TAPS, outs, chans), jnp.bfloat16),
            pltpu.VMEM(block, jnp.float32),
            pltpu.SemaphoreType.DMA((TAPS,)),
        ],
        compiler_params=pltpu.CompilerParams(vmem_limit_bytes=40 * 1024 * 1024),
        cost_estimate=pl.CostEstimate(
            flops=2 * frames * rows * padded * outs * chans * TAPS,
            bytes_accessed=2 * (TAPS * outs * chans + act.size),
            transcendentals=0,
        ),
    )(place, act, weight)


def tail_kernel(
    parts_ref, skip_ref, inside_ref, bias_ref, pick_ref, upper_ref, up_bias_ref, order_ref,
    out_ref, tap_ref, fine_ref, all_ref,
):
    frames, fine_rows, fine_cols, outs = out_ref.shape
    rows, cols = fine_rows // 2, fine_cols // 2
    wide = cols + 2
    summed = skip_ref[...].astype(jnp.float32) + bias_ref[...]
    for parity in range(2):
        total = parts_ref[4 * parity].astype(jnp.float32)
        for quarter in range(1, 4):
            total = total + parts_ref[4 * parity + quarter].astype(jnp.float32)
        upper_half = total.astype(jnp.bfloat16)
        lower_half = (total - upper_half.astype(jnp.float32)).astype(jnp.bfloat16)
        for part in (lower_half, upper_half):
            summed = summed + jnp.dot(part, pick_ref[parity], preferred_element_type=jnp.float32)
    summed = jnp.where(inside_ref[...] > 0.0, summed, 0.0).astype(jnp.bfloat16)
    held = outs // upper_ref.shape[1]
    for tap in range(9):
        weight = upper_ref[tap * held : (tap + 1) * held].reshape(outs, -1)
        tap_ref[tap] = lax.dot_general(summed, weight, NT, preferred_element_type=jnp.float32)

    spare = jnp.zeros((cols, 256 - outs), jnp.float32)
    for frame in range(frames):
        for row in range(rows):
            for low in range(2):
                lines = []
                for dx in range(3):
                    line = up_bias_ref[...] if dx == 1 else 0.0
                    for dy in range(3):
                        at = row + (low + dy - 1) // 2
                        if 0 <= at < rows:
                            at = (frame * rows + at) * wide
                            line = line + tap_ref[3 * dy + dx, at : at + wide, :]
                    lines.append(line)
                left = lines[0][0:cols] + (lines[1] + lines[2])[1 : 1 + cols]
                right = (lines[0] + lines[1])[1 : 1 + cols] + lines[2][2 : 2 + cols]
                for side, value in ((0, left), (1, right)):
                    fine_ref[0, pl.ds(side, cols, stride=2), :] = value[:, :128]
                    fine_ref[1, pl.ds(side, cols, stride=2), :] = jnp.concatenate([value[:, 128:], spare], axis=1)
                at = (frame * fine_rows + 2 * row + low) * fine_cols
                all_ref[at : at + fine_cols, 0:128] = fine_ref[0].astype(jnp.bfloat16)
                all_ref[at : at + fine_cols, 128:256] = fine_ref[1].astype(jnp.bfloat16)
    result = jnp.dot(all_ref[...], order_ref[...], preferred_element_type=jnp.float32)
    out_ref[...] = result.astype(out_ref.dtype).reshape(out_ref.shape)


def tail(parts, skip, inside, bias, pick, upper, up_bias, order, shape):
    frames, fine_rows, fine_cols, outs = shape
    vmem = pl.BlockSpec(memory_space=pltpu.VMEM)
    return pl.pallas_call(
        tail_kernel,
        out_shape=jax.ShapeDtypeStruct(shape, jnp.bfloat16),
        in_specs=[vmem] * 8,
        out_specs=vmem,
        scratch_shapes=[
            pltpu.VMEM((9, skip.shape[0], outs), jnp.float32),
            pltpu.VMEM((2, fine_cols, 128), jnp.float32),
            pltpu.VMEM((frames * fine_rows * fine_cols, 256), jnp.bfloat16),
        ],
        compiler_params=pltpu.CompilerParams(vmem_limit_bytes=40 * 1024 * 1024),
        cost_estimate=pl.CostEstimate(
            flops=2 * skip.shape[0] * upper.size, bytes_accessed=2 * upper.size, transcendentals=0
        ),
    )(parts, skip, inside, bias, pick, upper, up_bias, order)


def per_device(sizes, features, skip, norm_gain, norm_bias, conv_weight, conv_bias, up_weight, up_bias):
    frames, rows, cols, chans = features.shape
    pairs = sizes["m"]
    strips = sizes["x"] * sizes["y1"] * 4
    columns = strips * cols
    quarter = 2 * lax.axis_index("y0") + lax.axis_index("c")
    quad = lax.axis_index("x") * sizes["y1"] + lax.axis_index("y1")
    strip = 4 * quad + quarter
    even = lax.axis_index("p") == 0

    shard, up_shard = conv_weight.shape[0], up_weight.shape[0]
    mine = lax.dynamic_slice_in_dim(conv_weight, jnp.minimum(quarter * TAPS, 27 - TAPS - 1), TAPS + 1, axis=1)
    gathered = lax.all_gather(mine, "m", axis=0, tiled=True).transpose(1, 0, 2)

    planes = 2 * pairs
    outs = up_shard * planes
    share = next(r for r in range(1, up_shard + 1) if up_shard % r == 0 and 9 * up_shard // r <= strips)
    held_rows = up_weight.transpose(1, 0, 2).reshape(9 * up_shard, chans)
    up_mine = lax.dynamic_slice_in_dim(held_rows, jnp.minimum(strip * share, 9 * up_shard - share), share, axis=0)
    up_mine = handed_out(up_mine, TIME, planes).reshape(planes * share, chans)

    other = swap(features, "p")
    eight = jnp.concatenate([jnp.where(even, features, other), jnp.where(even, other, features)], axis=0)
    back = lax.ppermute(eight[2 * frames - 2 :], "m", [(i, i + 1) for i in range(pairs - 1)])
    ten = jnp.concatenate([back, eight], axis=0)
    by_y = swap(ten, "y0")
    everyone = handed_out(local_stats(ten), TILE, strips)
    up_mine, everyone = lax.optimization_barrier((up_mine, everyone))
    upper = handed_out(up_mine, TILE, strips)

    by_c = swap(jnp.stack([ten, by_y]), "c")
    held = (ten, by_c[0], by_y, by_c[1])
    head, tail_end = held[0][:, :, :2], held[0][:, :, cols - 2 :]
    for flip in range(1, 4):
        head = jnp.where(quarter == flip, held[flip][:, :, :2], head)
        tail_end = jnp.where(quarter == 3 - flip, held[flip][:, :, cols - 2 :], tail_end)
    skip_left = strip_shift(skip[:, :, cols - 1 :], strips, 1)
    skip_right = strip_shift(skip[:, :, :1], strips, -1)
    skip_left, skip_right, head, tail_end = lax.optimization_barrier((skip_left, skip_right, head, tail_end))
    left = strip_shift(tail_end, strips, 4)
    right = strip_shift(head, strips, -4)
    skip10 = jnp.concatenate([skip_left, skip, skip_right], axis=2).reshape(-1, chans)
    column = strip * cols - 1 + jnp.arange(skip10.shape[0]) % (cols + 2)
    inside = jnp.logical_and(column >= 0, column < columns).astype(jnp.float32)[:, None]

    width = chans // GROUPS
    mean, scale = whole_stats(everyone, float(rows * cols * width))
    mean = jnp.repeat(mean, width, axis=1)
    scale = jnp.repeat(scale, width, axis=1)
    place = jnp.stack([quad * 4 * cols - 2, lax.axis_index("m"), quarter])
    act = activate(
        place, (ten, by_y, by_c[0], by_c[1]), left, right, mean, scale, norm_gain, norm_bias, columns
    )

    gathered, act, skip10 = lax.optimization_barrier((gathered, act, skip10))
    last = (quarter == 3).astype(jnp.int32)
    parts = conv_partial(jnp.stack([jnp.minimum(quarter * TAPS, 27 - TAPS), last]), act, gathered, cols + 2)

    channel = jnp.arange(chans).reshape(pairs, 2, shard).transpose(1, 0, 2).reshape(2, chans // 2)
    pick = (channel[:, :, None] == jnp.arange(chans)[None, None, :]).astype(jnp.bfloat16)
    gathered_as = (planes, up_shard // share, share)
    out_channel = jnp.arange(outs).reshape(gathered_as).transpose(1, 0, 2).reshape(outs)
    order = jnp.pad(out_channel, (0, 256 - outs), constant_values=-1)[:, None] == jnp.arange(outs)[None, :]
    up_bias = up_bias.reshape(gathered_as).transpose(1, 0, 2).reshape(1, outs)
    parts = lax.all_to_all(parts, TEAM, 0, 0, tiled=True)
    return tail(
        parts, skip10, inside, conv_bias[None], pick, upper.reshape(strips, planes * share, chans),
        up_bias, order.astype(jnp.bfloat16), (frames, 2 * rows, 2 * cols, outs),
    )


def solution(mesh):
    strips = mesh.shape["tile"]
    side = 2
    while side * side * 2 < strips:
        side *= 2
    sizes = {"m": mesh.shape["tm"] // 2, "p": 2, "x": strips // (2 * side), "y1": side // 2, "y0": 2, "c": 2}
    fine_mesh = Mesh(mesh.devices.reshape(tuple(sizes.values())), tuple(sizes))

    def body(*arrays):
        return per_device(sizes, *arrays)

    return jax.shard_map(
        body,
        mesh=fine_mesh,
        in_specs=(
            P(TIME, None, TILE, None),
            P(TIME, None, TILE, None),
            P(),
            P(),
            P(TIME, None, None),
            P(),
            P(TIME, None, None),
            P(),
        ),
        out_specs=P(TIME, None, TILE, None),
        check_vma=False,
    )
```

```python
import jax
import jax.numpy as jnp
from jax import lax
from jax.experimental import pallas as pl
from jax.experimental.pallas import tpu as pltpu
from jax.sharding import Mesh
from jax.sharding import PartitionSpec as P

GROUPS = 32
EPSILON = 1e-06
TIME = ("m", "p")
TILE = ("x", "y1", "y0", "c")
TEAM = ("p", "y0", "c")
CHIPS = ("p", "x", "y1", "y0")
TAPS = 7
PADDED = 48
NT = (((1,), (1,)), ((), ()))


def swap(array, axis):
    return lax.ppermute(array, axis, [(0, 1), (1, 0)])


def strip_shift(array, count, by):
    return lax.ppermute(array, TILE, [(i, i + by) for i in range(count) if 0 <= i + by < count])


def handed_out(array, axes, members):
    return lax.all_to_all(jnp.broadcast_to(array[None], (members,) + array.shape), axes, 0, 0, tiled=True)


def local_stats(values):
    frames, rows, cols, chans = values.shape
    width = chans // GROUPS
    values = values.astype(jnp.float32)
    chan_mean = jnp.mean(values, axis=(1, 2))
    centered = values - chan_mean[:, None, None, :]
    chan_m2 = jnp.sum(centered * centered, axis=(1, 2))
    chan_mean = chan_mean.reshape(frames, GROUPS, width)
    mean = jnp.mean(chan_mean, axis=2)
    apart = chan_mean - mean[:, :, None]
    m2 = jnp.sum(chan_m2.reshape(frames, GROUPS, width) + rows * cols * apart * apart, axis=2)
    return jnp.concatenate([mean, m2], axis=1)


def whole_stats(everyone, members):
    means, m2s = everyone[:, :, :GROUPS], everyone[:, :, GROUPS:]
    mean = jnp.mean(means, axis=0)
    apart = means - mean
    m2 = jnp.sum(m2s + members * apart * apart, axis=0)
    return mean, lax.rsqrt(m2 / (members * everyone.shape[0]) + EPSILON)


def act_kernel(
    place_ref, own_ref, by_y_ref, by_c_ref, left_ref, right_ref, mean_ref, scale_ref, gain_ref, bias_ref,
    out_ref, done_ref, slab_ref, *, columns,
):
    frames, rows, cols, chans = own_ref.shape
    padded = slab_ref.shape[0]
    first, pair, quarter = place_ref[0], place_ref[1], place_ref[2]
    column = first - 6 + lax.broadcasted_iota(jnp.int32, (padded, chans), 0)
    inside = jnp.logical_and(column >= 0, column < columns)
    slab_ref[...] = jnp.zeros_like(slab_ref)
    done_ref[...] = jnp.zeros_like(done_ref)
    nothing = jnp.zeros((padded, chans), out_ref.dtype)

    def one_frame(frame, carry):
        keep = jnp.logical_and(inside, jnp.logical_or(pair > 0, frame >= 2))
        gain = scale_ref[frame] * gain_ref[...]
        for dx in range(3):
            out_ref[dx, frame, 0] = nothing
            out_ref[dx, frame, rows + 1] = nothing
        for row in range(rows):
            for flip, strip in enumerate((own_ref, by_c_ref.at[0], by_y_ref, by_c_ref.at[1])):
                at = pl.multiple_of(8 + cols * jnp.bitwise_xor(quarter, flip), 8)
                slab_ref[pl.ds(at, cols), :] = strip[frame, row].astype(jnp.float32)
            slab_ref[6:8, :] = left_ref[frame, row].astype(jnp.float32)
            slab_ref[8 + 4 * cols : 10 + 4 * cols, :] = right_ref[frame, row].astype(jnp.float32)
            value = (slab_ref[...] - mean_ref[frame]) * gain + bias_ref[...]
            value = 0.5 * value
            value = jnp.where(keep, value + value * jnp.tanh(value), 0.0)
            for dx in range(3):
                out_ref[dx, frame, row + 1] = pltpu.roll(value, padded - 6 - dx, 0).astype(out_ref.dtype)
        return carry

    lax.fori_loop(0, frames, one_frame, 0)


def activate(place, own, by_y, by_c, left, right, mean, scale, gain, bias, columns):
    frames, rows, cols, chans = own.shape

    def kernel(*refs):
        act_kernel(*refs, columns=columns)

    vmem = pl.BlockSpec(memory_space=pltpu.VMEM)
    return pl.pallas_call(
        kernel,
        out_shape=(
            jax.ShapeDtypeStruct((3, frames, rows + 2, PADDED, chans), jnp.bfloat16),
            jax.ShapeDtypeStruct((8, 128), jnp.float32),
        ),
        in_specs=[pl.BlockSpec(memory_space=pltpu.SMEM)] + [vmem] * 9,
        out_specs=(vmem, vmem),
        scratch_shapes=[pltpu.VMEM((PADDED, chans), jnp.float32)],
        compiler_params=pltpu.CompilerParams(vmem_limit_bytes=40 * 1024 * 1024),
        cost_estimate=pl.CostEstimate(
            flops=100 * own.size, bytes_accessed=60 * own.size, transcendentals=6 * own.size
        ),
    )(place, own, by_y, by_c, left, right, mean[:, None], scale[:, None], gain[None], bias[None])


def conv_kernel(place_ref, act_ref, weight_ref, out_ref, held_ref, stage_ref):
    outs, chans = weight_ref.shape[1:]
    frames, rows, padded = act_ref.shape[1] - 2, act_ref.shape[2] - 2, act_ref.shape[3]
    members, span = out_ref.shape[0], frames // 2
    cols = out_ref.shape[1] // (span * rows)
    first, doubled = place_ref[0], place_ref[1]
    for i in range(TAPS):
        weight = weight_ref[i]
        if i == 0:
            weight = weight * (1.0 - doubled.astype(jnp.float32)).astype(weight.dtype)
        held_ref[i // 2, :, (i % 2) * chans : (i % 2 + 1) * chans] = weight

    def window(chunk, i):
        tap = first + i
        taken = act_ref[tap % 3, pl.ds(tap // 9 + chunk, 2), pl.ds(tap // 3 % 3, rows)]
        return taken.reshape(2 * rows * padded, chans)

    for chunk in range(0, frames, 2):
        total = None
        for pair in range((TAPS + 1) // 2):
            taken, weight = window(chunk, 2 * pair), held_ref[pair]
            if 2 * pair + 1 < TAPS:
                taken = jnp.concatenate([taken, window(chunk, 2 * pair + 1)], axis=1)
            else:
                weight = weight[:, :chans]
            part = lax.dot_general(taken, weight, NT, preferred_element_type=jnp.float32)
            total = part if pair == 0 else total + part
        total = total.reshape(2, rows, padded, outs)
        for step in range(2):
            plane, frame = (chunk + step) // span, (chunk + step) % span
            for row in range(rows):
                at = (frame * rows + row) * cols
                for strip in range(4):
                    stage_ref[4 * plane + strip, at : at + cols, :] = total[step, row, strip * 8 : strip * 8 + cols]
    for member in range(members):
        out_ref[member] = stage_ref[member].astype(out_ref.dtype)


def conv_partial(place, act, weight, cols):
    slots, outs, chans = weight.shape
    _, frames, rows, padded, _ = act.shape
    frames, rows = frames - 2, rows - 2
    block = (8, frames // 2 * rows * cols, outs)
    vmem = pl.BlockSpec(memory_space=pltpu.VMEM)
    return pl.pallas_call(
        conv_kernel,
        out_shape=jax.ShapeDtypeStruct(block, jnp.bfloat16),
        in_specs=[pl.BlockSpec(memory_space=pltpu.SMEM), vmem, vmem],
        out_specs=vmem,
        scratch_shapes=[
            pltpu.VMEM(((TAPS + 1) // 2, outs, 2 * chans), jnp.bfloat16),
            pltpu.VMEM(block, jnp.float32),
        ],
        compiler_params=pltpu.CompilerParams(vmem_limit_bytes=40 * 1024 * 1024),
        cost_estimate=pl.CostEstimate(
            flops=2 * frames * rows * padded * outs * chans * TAPS,
            bytes_accessed=2 * (TAPS * outs * chans + act.size),
            transcendentals=0,
        ),
    )(place, act, weight)


def tail_kernel(
    core_ref, parts_ref, skip_ref, inside_ref, bias_ref, pick_ref, upper_ref, upper_by_c_ref, up_bias_ref, order_ref,
    out_ref, tap_ref, fine_ref, all_ref,
):
    frames, fine_rows, fine_cols, outs = out_ref.shape
    rows, cols = fine_rows // 2, fine_cols // 2
    wide = cols + 2
    summed = skip_ref[...].astype(jnp.float32) + bias_ref[...]
    for parity in range(2):
        total = parts_ref[4 * parity].astype(jnp.float32)
        for quarter in range(1, 4):
            total = total + parts_ref[4 * parity + quarter].astype(jnp.float32)
        upper_half = total.astype(jnp.bfloat16)
        lower_half = (total - upper_half.astype(jnp.float32)).astype(jnp.bfloat16)
        for part in (lower_half, upper_half):
            summed = summed + jnp.dot(part, pick_ref[parity], preferred_element_type=jnp.float32)
    summed = jnp.where(inside_ref[...] > 0.0, summed, 0.0).astype(jnp.bfloat16)
    chips, held = upper_ref.shape[0] // 2, outs // (2 * upper_ref.shape[1])
    for tap in range(9):
        weight = []
        for group in range(tap * held, (tap + 1) * held):
            for parity in range(2):
                at = parity * chips + group // 2
                mine = core_ref[0] == group % 2
                weight.append(jnp.where(mine, upper_ref[at], upper_by_c_ref[at]))
        weight = jnp.concatenate(weight, axis=0)
        tap_ref[tap] = lax.dot_general(summed, weight, NT, preferred_element_type=jnp.float32)

    spare = jnp.zeros((cols, 256 - outs), jnp.float32)
    for frame in range(frames):
        for row in range(rows):
            for low in range(2):
                lines = []
                for dx in range(3):
                    line = up_bias_ref[...] if dx == 1 else 0.0
                    for dy in range(3):
                        at = row + (low + dy - 1) // 2
                        if 0 <= at < rows:
                            at = (frame * rows + at) * wide
                            line = line + tap_ref[3 * dy + dx, at : at + wide, :]
                    lines.append(line)
                left = lines[0][0:cols] + (lines[1] + lines[2])[1 : 1 + cols]
                right = (lines[0] + lines[1])[1 : 1 + cols] + lines[2][2 : 2 + cols]
                for side, value in ((0, left), (1, right)):
                    fine_ref[0, pl.ds(side, cols, stride=2), :] = value[:, :128]
                    fine_ref[1, pl.ds(side, cols, stride=2), :] = jnp.concatenate([value[:, 128:], spare], axis=1)
                at = (frame * fine_rows + 2 * row + low) * fine_cols
                all_ref[at : at + fine_cols, 0:128] = fine_ref[0].astype(jnp.bfloat16)
                all_ref[at : at + fine_cols, 128:256] = fine_ref[1].astype(jnp.bfloat16)
    result = jnp.dot(all_ref[...], order_ref[...], preferred_element_type=jnp.float32)
    out_ref[...] = result.astype(out_ref.dtype).reshape(out_ref.shape)


def tail(core, parts, skip, inside, bias, pick, upper, upper_by_c, up_bias, order, shape):
    frames, fine_rows, fine_cols, outs = shape
    vmem = pl.BlockSpec(memory_space=pltpu.VMEM)
    return pl.pallas_call(
        tail_kernel,
        out_shape=jax.ShapeDtypeStruct(shape, jnp.bfloat16),
        in_specs=[pl.BlockSpec(memory_space=pltpu.SMEM)] + [vmem] * 9,
        out_specs=vmem,
        scratch_shapes=[
            pltpu.VMEM((9, skip.shape[0], outs), jnp.float32),
            pltpu.VMEM((2, fine_cols, 128), jnp.float32),
            pltpu.VMEM((frames * fine_rows * fine_cols, 256), jnp.bfloat16),
        ],
        compiler_params=pltpu.CompilerParams(vmem_limit_bytes=40 * 1024 * 1024),
        cost_estimate=pl.CostEstimate(
            flops=2 * skip.shape[0] * upper.size, bytes_accessed=2 * upper.size, transcendentals=0
        ),
    )(core, parts, skip, inside, bias, pick, upper, upper_by_c, up_bias, order)


def per_device(sizes, features, skip, norm_gain, norm_bias, conv_weight, conv_bias, up_weight, up_bias):
    frames, rows, cols, chans = features.shape
    pairs = sizes["m"]
    strips = sizes["x"] * sizes["y1"] * 4
    columns = strips * cols
    quarter = 2 * lax.axis_index("y0") + lax.axis_index("c")
    quad = lax.axis_index("x") * sizes["y1"] + lax.axis_index("y1")
    strip = 4 * quad + quarter
    even = lax.axis_index("p") == 0

    shard, up_shard = conv_weight.shape[0], up_weight.shape[0]
    outs = up_shard * 2 * pairs
    first_tap = jnp.minimum(quarter * TAPS, 27 - TAPS)
    share = next(r for r in range(1, up_shard + 1) if up_shard % r == 0 and 9 * up_shard // r <= strips)
    up_rows = up_weight.transpose(1, 0, 2).reshape(9 * up_shard, chans)
    up_rows = lax.dynamic_slice_in_dim(up_rows, jnp.minimum(strip * share, 9 * up_shard - share), share, axis=0)
    mine = jnp.concatenate(
        [
            lax.dynamic_slice_in_dim(conv_weight, first_tap, TAPS, axis=1),
            jnp.pad(up_rows, ((0, shard - share), (0, 0)))[:, None],
        ],
        axis=1,
    )
    mine, features = lax.optimization_barrier((mine, features))
    gathered = lax.all_gather(mine, "m", axis=0, tiled=True).transpose(1, 0, 2)

    other = swap(features, "p")
    eight = jnp.concatenate([jnp.where(even, features, other), jnp.where(even, other, features)], axis=0)
    back = lax.ppermute(eight[2 * frames - 2 :], "m", [(i, i + 1) for i in range(pairs - 1)])
    ten = jnp.concatenate([back, eight], axis=0)
    by_y = swap(ten, "y0")
    everyone = handed_out(local_stats(ten), TILE, strips)

    by_c = swap(jnp.stack([ten, by_y]), "c")
    held = (ten, by_c[0], by_y, by_c[1])
    head, tail_end = held[0][:, :, :2], held[0][:, :, cols - 2 :]
    for flip in range(1, 4):
        head = jnp.where(quarter == flip, held[flip][:, :, :2], head)
        tail_end = jnp.where(quarter == 3 - flip, held[flip][:, :, cols - 2 :], tail_end)
    ending, start, head, tail_end = lax.optimization_barrier(
        (skip[:, :, cols - 1 :], skip[:, :, :1], head, tail_end)
    )
    left = strip_shift(tail_end, strips, 4)
    right = strip_shift(head, strips, -4)
    skip_left = strip_shift(ending, strips, 1)
    skip_right = strip_shift(start, strips, -1)
    left, right, skip_left, skip_right = lax.optimization_barrier((left, right, skip_left, skip_right))
    skip10 = jnp.concatenate([skip_left, skip, skip_right], axis=2).reshape(-1, chans)
    column = strip * cols - 1 + jnp.arange(skip10.shape[0]) % (cols + 2)
    inside = jnp.logical_and(column >= 0, column < columns).astype(jnp.float32)[:, None]

    width = chans // GROUPS
    mean, scale = whole_stats(everyone, float(rows * cols * width))
    mean = jnp.repeat(mean, width, axis=1)
    scale = jnp.repeat(scale, width, axis=1)
    place = jnp.stack([quad * 4 * cols - 2, lax.axis_index("m"), quarter])
    act, done = activate(place, ten, by_y, by_c, left, right, mean, scale, norm_gain, norm_bias, columns)

    gathered, done = lax.optimization_barrier((gathered, done))
    up_rows = gathered[TAPS].reshape(pairs, shard, chans)[:, :share].reshape(pairs * share, chans)
    upper = handed_out(up_rows, CHIPS, strips)
    last = (quarter == 3).astype(jnp.int32)
    parts = conv_partial(jnp.stack([first_tap, last]), act, gathered, cols + 2)
    upper = upper.reshape(strips, pairs * share, chans)
    upper_by_c = swap(upper, "c")

    channel = jnp.arange(chans).reshape(pairs, 2, shard).transpose(1, 0, 2).reshape(2, chans // 2)
    pick = (channel[:, :, None] == jnp.arange(chans)[None, None, :]).astype(jnp.bfloat16)
    gathered_as, turn = (pairs, 2, up_shard // share, share), (2, 1, 0, 3)
    out_channel = jnp.arange(outs).reshape(gathered_as).transpose(turn).reshape(outs)
    order = jnp.pad(out_channel, (0, 256 - outs), constant_values=-1)[:, None] == jnp.arange(outs)[None, :]
    up_bias = up_bias.reshape(gathered_as).transpose(turn).reshape(1, outs)
    parts = lax.all_to_all(parts, TEAM, 0, 0, tiled=True)
    return tail(
        lax.axis_index("c").reshape(1), parts, skip10, inside, conv_bias[None], pick, upper, upper_by_c,
        up_bias, order.astype(jnp.bfloat16), (frames, 2 * rows, 2 * cols, outs),
    )


def solution(mesh):
    strips = mesh.shape["tile"]
    side = 2
    while side * side * 2 < strips:
        side *= 2
    sizes = {"m": mesh.shape["tm"] // 2, "p": 2, "x": strips // (2 * side), "y1": side // 2, "y0": 2, "c": 2}
    fine_mesh = Mesh(mesh.devices.reshape(tuple(sizes.values())), tuple(sizes))

    def body(*arrays):
        return per_device(sizes, *arrays)

    return jax.shard_map(
        body,
        mesh=fine_mesh,
        in_specs=(
            P(TIME, None, TILE, None),
            P(TIME, None, TILE, None),
            P(),
            P(),
            P(TIME, None, None),
            P(),
            P(TIME, None, None),
            P(),
        ),
        out_specs=P(TIME, None, TILE, None),
        check_vma=False,
    )
```

```python
import jax
import jax.numpy as jnp
from jax import lax
from jax.experimental import pallas as pl
from jax.experimental.pallas import tpu as pltpu
from jax.sharding import Mesh
from jax.sharding import PartitionSpec as P

GROUPS = 32
EPSILON = 1e-06
TIME = ("m", "p")
TILE = ("x", "y1", "y0", "c")
TEAM = ("p", "y0", "c")
CHIPS = ("p", "x", "y1", "y0")
TAPS = 7
PADDED = 48
NT = (((1,), (1,)), ((), ()))


def swap(array, axis):
    return lax.ppermute(array, axis, [(0, 1), (1, 0)])


def strip_shift(array, count, by):
    return lax.ppermute(array, TILE, [(i, i + by) for i in range(count) if 0 <= i + by < count])


def handed_out(array, axes, members):
    return lax.all_to_all(jnp.broadcast_to(array[None], (members,) + array.shape), axes, 0, 0, tiled=True)


def local_stats(values):
    frames, rows, cols, chans = values.shape
    width = chans // GROUPS
    values = values.astype(jnp.float32)
    chan_mean = jnp.mean(values, axis=(1, 2))
    centered = values - chan_mean[:, None, None, :]
    chan_m2 = jnp.sum(centered * centered, axis=(1, 2))
    chan_mean = chan_mean.reshape(frames, GROUPS, width)
    mean = jnp.mean(chan_mean, axis=2)
    apart = chan_mean - mean[:, :, None]
    m2 = jnp.sum(chan_m2.reshape(frames, GROUPS, width) + rows * cols * apart * apart, axis=2)
    return jnp.pad(jnp.concatenate([mean, m2], axis=1), ((0, -frames % 8), (0, 128 - 2 * GROUPS)))


def chan_stats(everyone, chans, members):
    strips = everyone.shape[0]
    sums = jnp.sum(everyone, axis=0)
    mean = sums / strips
    apart = everyone - mean[None]
    between = jnp.sum(apart * apart, axis=0)
    lane = lax.broadcasted_iota(jnp.int32, (128, chans), 0)
    chan = lax.broadcasted_iota(jnp.int32, (128, chans), 1)
    width = chans // GROUPS

    def widened(values, first):
        low = (lane - first) * width
        pick = jnp.logical_and(chan >= low, chan < low + width).astype(jnp.float32)
        return jnp.dot(values, pick, precision=lax.Precision.HIGHEST, preferred_element_type=jnp.float32)

    spread = (widened(sums, GROUPS) + members * widened(between, 0)) / (members * strips)
    return widened(mean, 0), lax.rsqrt(spread + EPSILON)


def act_kernel(
    place_ref, own_ref, by_y_ref, by_c_ref, left_ref, right_ref, stats_ref, gain_ref, bias_ref,
    out_ref, done_ref, slab_ref, mean_ref, scale_ref, *, columns,
):
    frames, rows, cols, chans = own_ref.shape
    padded = slab_ref.shape[0]
    first, pair, quarter = place_ref[0], place_ref[1], place_ref[2]
    column = first - 6 + lax.broadcasted_iota(jnp.int32, (padded, chans), 0)
    inside = jnp.logical_and(column >= 0, column < columns)
    mean_ref[...], scale_ref[...] = chan_stats(stats_ref[...], chans, float(rows * cols * (chans // GROUPS)))
    scale_ref[...] *= gain_ref[...]
    slab_ref[...] = jnp.zeros_like(slab_ref)
    done_ref[...] = jnp.zeros_like(done_ref)
    nothing = jnp.zeros((padded, chans), out_ref.dtype)

    def one_frame(frame, carry):
        keep = jnp.logical_and(inside, jnp.logical_or(pair > 0, frame >= 2))
        mean, gain = mean_ref[pl.ds(frame, 1), :], scale_ref[pl.ds(frame, 1), :]
        for dx in range(3):
            out_ref[dx, frame, 0] = nothing
            out_ref[dx, frame, rows + 1] = nothing
        for row in range(rows):
            for flip, strip in enumerate((own_ref, by_c_ref.at[0], by_y_ref, by_c_ref.at[1])):
                at = pl.multiple_of(8 + cols * jnp.bitwise_xor(quarter, flip), 8)
                slab_ref[pl.ds(at, cols), :] = strip[frame, row].astype(jnp.float32)
            slab_ref[6:8, :] = left_ref[frame, row].astype(jnp.float32)
            slab_ref[8 + 4 * cols : 10 + 4 * cols, :] = right_ref[frame, row].astype(jnp.float32)
            value = (slab_ref[...] - mean) * gain + bias_ref[...]
            value = 0.5 * value
            value = jnp.where(keep, value + value * jnp.tanh(value), 0.0)
            for dx in range(3):
                out_ref[dx, frame, row + 1] = pltpu.roll(value, padded - 6 - dx, 0).astype(out_ref.dtype)
        return carry

    lax.fori_loop(0, frames, one_frame, 0)


def activate(place, own, by_y, by_c, left, right, stats, gain, bias, columns):
    frames, rows, cols, chans = own.shape

    def kernel(*refs):
        act_kernel(*refs, columns=columns)

    vmem = pl.BlockSpec(memory_space=pltpu.VMEM)
    return pl.pallas_call(
        kernel,
        out_shape=(
            jax.ShapeDtypeStruct((3, frames, rows + 2, PADDED, chans), jnp.bfloat16),
            jax.ShapeDtypeStruct((8, 128), jnp.float32),
        ),
        in_specs=[pl.BlockSpec(memory_space=pltpu.SMEM)] + [vmem] * 8,
        out_specs=(vmem, vmem),
        scratch_shapes=[
            pltpu.VMEM((PADDED, chans), jnp.float32),
            pltpu.VMEM((stats.shape[1], chans), jnp.float32),
            pltpu.VMEM((stats.shape[1], chans), jnp.float32),
        ],
        compiler_params=pltpu.CompilerParams(vmem_limit_bytes=40 * 1024 * 1024),
        cost_estimate=pl.CostEstimate(
            flops=100 * own.size, bytes_accessed=60 * own.size, transcendentals=6 * own.size
        ),
    )(place, own, by_y, by_c, left, right, stats, gain[None], bias[None])


def conv_kernel(place_ref, act_ref, weight_ref, out_ref, held_ref, stage_ref):
    outs, chans = weight_ref.shape[1:]
    frames, rows, padded = act_ref.shape[1] - 2, act_ref.shape[2] - 2, act_ref.shape[3]
    members, span = out_ref.shape[0], frames // 2
    cols = out_ref.shape[1] // (span * rows)
    first, doubled = place_ref[0], place_ref[1]
    for i in range(TAPS):
        weight = weight_ref[i]
        if i == 0:
            weight = weight * (1.0 - doubled.astype(jnp.float32)).astype(weight.dtype)
        held_ref[i // 2, :, (i % 2) * chans : (i % 2 + 1) * chans] = weight

    def window(chunk, i):
        tap = first + i
        taken = act_ref[tap % 3, pl.ds(tap // 9 + chunk, 2), pl.ds(tap // 3 % 3, rows)]
        return taken.reshape(2 * rows * padded, chans)

    for chunk in range(0, frames, 2):
        total = None
        for pair in range((TAPS + 1) // 2):
            taken, weight = window(chunk, 2 * pair), held_ref[pair]
            if 2 * pair + 1 < TAPS:
                taken = jnp.concatenate([taken, window(chunk, 2 * pair + 1)], axis=1)
            else:
                weight = weight[:, :chans]
            part = lax.dot_general(taken, weight, NT, preferred_element_type=jnp.float32)
            total = part if pair == 0 else total + part
        total = total.reshape(2, rows, padded, outs)
        for step in range(2):
            plane, frame = (chunk + step) // span, (chunk + step) % span
            for row in range(rows):
                at = (frame * rows + row) * cols
                for strip in range(4):
                    stage_ref[4 * plane + strip, at : at + cols, :] = total[step, row, strip * 8 : strip * 8 + cols]
    for member in range(members):
        out_ref[member] = stage_ref[member].astype(out_ref.dtype)


def conv_partial(place, act, weight, cols):
    slots, outs, chans = weight.shape
    _, frames, rows, padded, _ = act.shape
    frames, rows = frames - 2, rows - 2
    block = (8, frames // 2 * rows * cols, outs)
    vmem = pl.BlockSpec(memory_space=pltpu.VMEM)
    return pl.pallas_call(
        conv_kernel,
        out_shape=jax.ShapeDtypeStruct(block, jnp.bfloat16),
        in_specs=[pl.BlockSpec(memory_space=pltpu.SMEM), vmem, vmem],
        out_specs=vmem,
        scratch_shapes=[
            pltpu.VMEM(((TAPS + 1) // 2, outs, 2 * chans), jnp.bfloat16),
            pltpu.VMEM(block, jnp.float32),
        ],
        compiler_params=pltpu.CompilerParams(vmem_limit_bytes=40 * 1024 * 1024),
        cost_estimate=pl.CostEstimate(
            flops=2 * frames * rows * padded * outs * chans * TAPS,
            bytes_accessed=2 * (TAPS * outs * chans + act.size),
            transcendentals=0,
        ),
    )(place, act, weight)


def tail_kernel(
    core_ref, parts_ref, skip_ref, inside_ref, bias_ref, pick_ref, upper_ref, upper_by_c_ref, up_bias_ref, order_ref,
    out_ref, tap_ref, fine_ref, all_ref,
):
    frames, fine_rows, fine_cols, outs = out_ref.shape
    rows, cols = fine_rows // 2, fine_cols // 2
    wide = cols + 2
    summed = skip_ref[...].astype(jnp.float32) + bias_ref[...]
    for parity in range(2):
        total = parts_ref[4 * parity].astype(jnp.float32)
        for quarter in range(1, 4):
            total = total + parts_ref[4 * parity + quarter].astype(jnp.float32)
        upper_half = total.astype(jnp.bfloat16)
        lower_half = (total - upper_half.astype(jnp.float32)).astype(jnp.bfloat16)
        for part in (lower_half, upper_half):
            summed = summed + jnp.dot(part, pick_ref[parity], preferred_element_type=jnp.float32)
    summed = jnp.where(inside_ref[...] > 0.0, summed, 0.0).astype(jnp.bfloat16)
    chips, held = upper_ref.shape[0] // 2, outs // (2 * upper_ref.shape[1])
    for tap in range(9):
        weight = []
        for group in range(tap * held, (tap + 1) * held):
            for parity in range(2):
                at = parity * chips + group // 2
                mine = core_ref[0] == group % 2
                weight.append(jnp.where(mine, upper_ref[at], upper_by_c_ref[at]))
        weight = jnp.concatenate(weight, axis=0)
        tap_ref[tap] = lax.dot_general(summed, weight, NT, preferred_element_type=jnp.float32)

    spare = jnp.zeros((cols, 256 - outs), jnp.float32)
    for frame in range(frames):
        for row in range(rows):
            for low in range(2):
                lines = []
                for dx in range(3):
                    line = up_bias_ref[...] if dx == 1 else 0.0
                    for dy in range(3):
                        at = row + (low + dy - 1) // 2
                        if 0 <= at < rows:
                            at = (frame * rows + at) * wide
                            line = line + tap_ref[3 * dy + dx, at : at + wide, :]
                    lines.append(line)
                left = lines[0][0:cols] + (lines[1] + lines[2])[1 : 1 + cols]
                right = (lines[0] + lines[1])[1 : 1 + cols] + lines[2][2 : 2 + cols]
                for side, value in ((0, left), (1, right)):
                    fine_ref[0, pl.ds(side, cols, stride=2), :] = value[:, :128]
                    fine_ref[1, pl.ds(side, cols, stride=2), :] = jnp.concatenate([value[:, 128:], spare], axis=1)
                at = (frame * fine_rows + 2 * row + low) * fine_cols
                all_ref[at : at + fine_cols, 0:128] = fine_ref[0].astype(jnp.bfloat16)
                all_ref[at : at + fine_cols, 128:256] = fine_ref[1].astype(jnp.bfloat16)
    result = jnp.dot(all_ref[...], order_ref[...], preferred_element_type=jnp.float32)
    out_ref[...] = result.astype(out_ref.dtype).reshape(out_ref.shape)


def tail(core, parts, skip, inside, bias, pick, upper, upper_by_c, up_bias, order, shape):
    frames, fine_rows, fine_cols, outs = shape
    vmem = pl.BlockSpec(memory_space=pltpu.VMEM)
    return pl.pallas_call(
        tail_kernel,
        out_shape=jax.ShapeDtypeStruct(shape, jnp.bfloat16),
        in_specs=[pl.BlockSpec(memory_space=pltpu.SMEM)] + [vmem] * 9,
        out_specs=vmem,
        scratch_shapes=[
            pltpu.VMEM((9, skip.shape[0], outs), jnp.float32),
            pltpu.VMEM((2, fine_cols, 128), jnp.float32),
            pltpu.VMEM((frames * fine_rows * fine_cols, 256), jnp.bfloat16),
        ],
        compiler_params=pltpu.CompilerParams(vmem_limit_bytes=40 * 1024 * 1024),
        cost_estimate=pl.CostEstimate(
            flops=2 * skip.shape[0] * upper.size, bytes_accessed=2 * upper.size, transcendentals=0
        ),
    )(core, parts, skip, inside, bias, pick, upper, upper_by_c, up_bias, order)


def per_device(sizes, features, skip, norm_gain, norm_bias, conv_weight, conv_bias, up_weight, up_bias):
    frames, rows, cols, chans = features.shape
    pairs = sizes["m"]
    strips = sizes["x"] * sizes["y1"] * 4
    columns = strips * cols
    quarter = 2 * lax.axis_index("y0") + lax.axis_index("c")
    quad = lax.axis_index("x") * sizes["y1"] + lax.axis_index("y1")
    strip = 4 * quad + quarter
    even = lax.axis_index("p") == 0

    shard, up_shard = conv_weight.shape[0], up_weight.shape[0]
    outs = up_shard * 2 * pairs
    first_tap = jnp.minimum(quarter * TAPS, 27 - TAPS)
    share = next(r for r in range(1, up_shard + 1) if up_shard % r == 0 and 9 * up_shard // r <= strips)
    up_rows = up_weight.transpose(1, 0, 2).reshape(9 * up_shard, chans)
    up_rows = lax.dynamic_slice_in_dim(up_rows, jnp.minimum(strip * share, 9 * up_shard - share), share, axis=0)
    mine = jnp.concatenate(
        [
            lax.dynamic_slice_in_dim(conv_weight, first_tap, TAPS, axis=1),
            jnp.pad(up_rows, ((0, shard - share), (0, 0)))[:, None],
        ],
        axis=1,
    )
    mine, features = lax.optimization_barrier((mine, features))
    gathered = lax.all_gather(mine, "m", axis=0, tiled=True).transpose(1, 0, 2)

    other = swap(features, "p")
    eight = jnp.concatenate([jnp.where(even, features, other), jnp.where(even, other, features)], axis=0)
    back = lax.ppermute(eight[2 * frames - 2 :], "m", [(i, i + 1) for i in range(pairs - 1)])
    ten = jnp.concatenate([back, eight], axis=0)
    by_y = swap(ten, "y0")
    everyone = handed_out(local_stats(ten), TILE, strips)

    by_c = swap(jnp.stack([ten, by_y]), "c")
    held = (ten, by_c[0], by_y, by_c[1])
    head, tail_end = held[0][:, :, :2], held[0][:, :, cols - 2 :]
    for flip in range(1, 4):
        head = jnp.where(quarter == flip, held[flip][:, :, :2], head)
        tail_end = jnp.where(quarter == 3 - flip, held[flip][:, :, cols - 2 :], tail_end)
    ending, start, head, tail_end = lax.optimization_barrier(
        (skip[:, :, cols - 1 :], skip[:, :, :1], head, tail_end)
    )
    left = strip_shift(tail_end, strips, 4)
    right = strip_shift(head, strips, -4)
    skip_left = strip_shift(ending, strips, 1)
    skip_right = strip_shift(start, strips, -1)
    left, right, skip_left, skip_right = lax.optimization_barrier((left, right, skip_left, skip_right))
    skip10 = jnp.concatenate([skip_left, skip, skip_right], axis=2).reshape(-1, chans)
    column = strip * cols - 1 + jnp.arange(skip10.shape[0]) % (cols + 2)
    inside = jnp.logical_and(column >= 0, column < columns).astype(jnp.float32)[:, None]

    place = jnp.stack([quad * 4 * cols - 2, lax.axis_index("m"), quarter])
    act, done = activate(place, ten, by_y, by_c, left, right, everyone, norm_gain, norm_bias, columns)

    up_rows = gathered[TAPS].reshape(pairs, shard, chans)[:, :share].reshape(pairs * share, chans)
    up_rows = (up_rows.astype(jnp.float32) + done[0, 0]).astype(jnp.bfloat16)
    upper = handed_out(up_rows, CHIPS, strips)
    last = (quarter == 3).astype(jnp.int32)
    parts = conv_partial(jnp.stack([first_tap, last]), act, gathered, cols + 2)
    upper = upper.reshape(strips, pairs * share, chans)
    upper_by_c = swap(upper, "c")

    channel = jnp.arange(chans).reshape(pairs, 2, shard).transpose(1, 0, 2).reshape(2, chans // 2)
    pick = (channel[:, :, None] == jnp.arange(chans)[None, None, :]).astype(jnp.bfloat16)
    gathered_as, turn = (pairs, 2, up_shard // share, share), (2, 1, 0, 3)
    out_channel = jnp.arange(outs).reshape(gathered_as).transpose(turn).reshape(outs)
    order = jnp.pad(out_channel, (0, 256 - outs), constant_values=-1)[:, None] == jnp.arange(outs)[None, :]
    up_bias = up_bias.reshape(gathered_as).transpose(turn).reshape(1, outs)
    parts = lax.all_to_all(parts, TEAM, 0, 0, tiled=True)
    return tail(
        lax.axis_index("c").reshape(1), parts, skip10, inside, conv_bias[None], pick, upper, upper_by_c,
        up_bias, order.astype(jnp.bfloat16), (frames, 2 * rows, 2 * cols, outs),
    )


def solution(mesh):
    strips = mesh.shape["tile"]
    side = 2
    while side * side * 2 < strips:
        side *= 2
    sizes = {"m": mesh.shape["tm"] // 2, "p": 2, "x": strips // (2 * side), "y1": side // 2, "y0": 2, "c": 2}
    fine_mesh = Mesh(mesh.devices.reshape(tuple(sizes.values())), tuple(sizes))

    def body(*arrays):
        return per_device(sizes, *arrays)

    return jax.shard_map(
        body,
        mesh=fine_mesh,
        in_specs=(
            P(TIME, None, TILE, None),
            P(TIME, None, TILE, None),
            P(),
            P(),
            P(TIME, None, None),
            P(),
            P(TIME, None, None),
            P(),
        ),
        out_specs=P(TIME, None, TILE, None),
        check_vma=False,
    )
```

```python
import jax
import jax.numpy as jnp
from jax import lax
from jax.experimental import pallas as pl
from jax.experimental.pallas import tpu as pltpu
from jax.sharding import Mesh
from jax.sharding import PartitionSpec as P

GROUPS = 32
EPSILON = 1e-06
TIME = ("m", "p")
TILE = ("x", "y1", "y0", "c")
TEAM = ("p", "y0", "c")
TAPS = 7
PADDED = 48
NT = (((1,), (1,)), ((), ()))


def swap(array, axis):
    return lax.ppermute(array, axis, [(0, 1), (1, 0)])


def strip_shift(array, count, by):
    return lax.ppermute(array, TILE, [(i, i + by) for i in range(count) if 0 <= i + by < count])


def handed_out(array, axes, members):
    return lax.all_to_all(jnp.broadcast_to(array[None], (members,) + array.shape), axes, 0, 0, tiled=True)


def local_stats(values):
    frames, rows, cols, chans = values.shape
    width = chans // GROUPS
    values = values.astype(jnp.float32)
    chan_mean = jnp.mean(values, axis=(1, 2))
    centered = values - chan_mean[:, None, None, :]
    chan_m2 = jnp.sum(centered * centered, axis=(1, 2))
    chan_mean = chan_mean.reshape(frames, GROUPS, width)
    mean = jnp.mean(chan_mean, axis=2)
    apart = chan_mean - mean[:, :, None]
    m2 = jnp.sum(chan_m2.reshape(frames, GROUPS, width) + rows * cols * apart * apart, axis=2)
    return jnp.pad(jnp.concatenate([mean, m2], axis=1), ((0, -frames % 8), (0, 128 - 2 * GROUPS)))


def chan_stats(everyone, chans, members):
    strips = everyone.shape[0]
    sums = jnp.sum(everyone, axis=0)
    mean = sums / strips
    apart = everyone - mean[None]
    between = jnp.sum(apart * apart, axis=0)
    lane = lax.broadcasted_iota(jnp.int32, (128, chans), 0)
    chan = lax.broadcasted_iota(jnp.int32, (128, chans), 1)
    width = chans // GROUPS

    def widened(values, first):
        low = (lane - first) * width
        pick = jnp.logical_and(chan >= low, chan < low + width).astype(jnp.float32)
        return jnp.dot(values, pick, precision=lax.Precision.HIGHEST, preferred_element_type=jnp.float32)

    spread = (widened(sums, GROUPS) + members * widened(between, 0)) / (members * strips)
    return widened(mean, 0), lax.rsqrt(spread + EPSILON)


def conv_kernel(
    place_ref, own_ref, by_y_ref, by_c_ref, left_ref, right_ref, stats_ref, gain_ref, bias_ref, weight_ref,
    out_ref, act_ref, slab_ref, mean_ref, scale_ref, held_ref, stage_ref, *, columns,
):
    frames, rows, cols, chans = own_ref.shape
    padded = slab_ref.shape[0]
    outs = weight_ref.shape[1]
    members, span = out_ref.shape[0], (frames - 2) // 2
    wide = cols + 2
    first, pair, quarter, first_tap, doubled = [place_ref[i] for i in range(5)]

    column = first - 6 + lax.broadcasted_iota(jnp.int32, (padded, chans), 0)
    inside = jnp.logical_and(column >= 0, column < columns)
    mean_ref[...], scale_ref[...] = chan_stats(stats_ref[...], chans, float(rows * cols * (chans // GROUPS)))
    scale_ref[...] *= gain_ref[...]
    slab_ref[...] = jnp.zeros_like(slab_ref)
    nothing = jnp.zeros((padded, chans), act_ref.dtype)

    def one_frame(frame, carry):
        keep = jnp.logical_and(inside, jnp.logical_or(pair > 0, frame >= 2))
        mean, gain = mean_ref[pl.ds(frame, 1), :], scale_ref[pl.ds(frame, 1), :]
        for dx in range(3):
            act_ref[dx, frame, 0] = nothing
            act_ref[dx, frame, rows + 1] = nothing
        for row in range(rows):
            for flip, strip in enumerate((own_ref, by_c_ref.at[0], by_y_ref, by_c_ref.at[1])):
                at = pl.multiple_of(8 + cols * jnp.bitwise_xor(quarter, flip), 8)
                slab_ref[pl.ds(at, cols), :] = strip[frame, row].astype(jnp.float32)
            slab_ref[6:8, :] = left_ref[frame, row].astype(jnp.float32)
            slab_ref[8 + 4 * cols : 10 + 4 * cols, :] = right_ref[frame, row].astype(jnp.float32)
            value = (slab_ref[...] - mean) * gain + bias_ref[...]
            value = 0.5 * value
            value = jnp.where(keep, value + value * jnp.tanh(value), 0.0)
            for dx in range(3):
                act_ref[dx, frame, row + 1] = pltpu.roll(value, padded - 6 - dx, 0).astype(act_ref.dtype)
        return carry

    lax.fori_loop(0, frames, one_frame, 0)

    for i in range(TAPS):
        weight = weight_ref[i]
        if i == 0:
            weight = weight * (1.0 - doubled.astype(jnp.float32)).astype(weight.dtype)
        held_ref[i // 2, :, (i % 2) * chans : (i % 2 + 1) * chans] = weight

    def window(chunk, i):
        tap = first_tap + i
        taken = act_ref[tap % 3, pl.ds(tap // 9 + chunk, 2), pl.ds(tap // 3 % 3, rows)]
        return taken.reshape(2 * rows * padded, chans)

    for chunk in range(0, frames - 2, 2):
        total = None
        for both in range((TAPS + 1) // 2):
            taken, weight = window(chunk, 2 * both), held_ref[both]
            if 2 * both + 1 < TAPS:
                taken = jnp.concatenate([taken, window(chunk, 2 * both + 1)], axis=1)
            else:
                weight = weight[:, :chans]
            part = lax.dot_general(taken, weight, NT, preferred_element_type=jnp.float32)
            total = part if both == 0 else total + part
        total = total.reshape(2, rows, padded, outs)
        for step in range(2):
            plane, frame = (chunk + step) // span, (chunk + step) % span
            for row in range(rows):
                at = (frame * rows + row) * wide
                for strip in range(4):
                    stage_ref[4 * plane + strip, at : at + wide, :] = total[step, row, strip * 8 : strip * 8 + wide]
    for member in range(members):
        out_ref[member] = stage_ref[member].astype(out_ref.dtype)


def conv_partial(place, own, by_y, by_c, left, right, stats, gain, bias, weight, columns):
    frames, rows, cols, chans = own.shape
    outs = weight.shape[1]
    block = (8, (frames - 2) // 2 * rows * (cols + 2), outs)

    def kernel(*refs):
        conv_kernel(*refs, columns=columns)

    vmem = pl.BlockSpec(memory_space=pltpu.VMEM)
    return pl.pallas_call(
        kernel,
        out_shape=jax.ShapeDtypeStruct(block, jnp.bfloat16),
        in_specs=[pl.BlockSpec(memory_space=pltpu.SMEM)] + [vmem] * 9,
        out_specs=vmem,
        scratch_shapes=[
            pltpu.VMEM((3, frames, rows + 2, PADDED, chans), jnp.bfloat16),
            pltpu.VMEM((PADDED, chans), jnp.float32),
            pltpu.VMEM((stats.shape[1], chans), jnp.float32),
            pltpu.VMEM((stats.shape[1], chans), jnp.float32),
            pltpu.VMEM(((TAPS + 1) // 2, outs, 2 * chans), jnp.bfloat16),
            pltpu.VMEM(block, jnp.float32),
        ],
        compiler_params=pltpu.CompilerParams(vmem_limit_bytes=40 * 1024 * 1024),
        cost_estimate=pl.CostEstimate(
            flops=2 * (frames - 2) * rows * PADDED * outs * chans * TAPS,
            bytes_accessed=2 * (TAPS * outs * chans + 8 * own.size),
            transcendentals=6 * own.size,
        ),
    )(place, own, by_y, by_c, left, right, stats, gain[None], bias[None], weight)


def order_kernel(turn_ref, own_ref, by_c_ref, out_ref, stage_ref):
    held = stage_ref.shape[1] // 8
    for core, ref in enumerate((own_ref, by_c_ref)):
        for k in range(4):
            rows = jnp.dot(turn_ref[...], ref[k], preferred_element_type=jnp.float32)
            at = (4 * core + k) * held
            for tap in range(9):
                stage_ref[tap, at : at + held, :] = rows[tap * held : (tap + 1) * held]
    for tap in range(9):
        out_ref[tap] = stage_ref[tap].astype(out_ref.dtype)


def in_order(turn, own, by_c, outs):
    vmem = pl.BlockSpec(memory_space=pltpu.VMEM)
    shape = (9, outs, own.shape[-1])
    return pl.pallas_call(
        order_kernel,
        out_shape=jax.ShapeDtypeStruct(shape, jnp.bfloat16),
        in_specs=[vmem] * 3,
        out_specs=vmem,
        scratch_shapes=[pltpu.VMEM(shape, jnp.float32)],
        compiler_params=pltpu.CompilerParams(vmem_limit_bytes=40 * 1024 * 1024),
        cost_estimate=pl.CostEstimate(flops=16 * turn.size * own.shape[-1], bytes_accessed=6 * own.size, transcendentals=0),
    )(turn, own, by_c)


def tail_kernel(
    parts_ref, skip_ref, inside_ref, bias_ref, pick_ref, upper_ref, up_bias_ref, order_ref,
    out_ref, tap_ref, fine_ref, all_ref,
):
    frames, fine_rows, fine_cols, outs = out_ref.shape
    rows, cols = fine_rows // 2, fine_cols // 2
    wide = cols + 2
    summed = skip_ref[...].astype(jnp.float32) + bias_ref[...]
    for parity in range(2):
        total = parts_ref[4 * parity].astype(jnp.float32)
        for quarter in range(1, 4):
            total = total + parts_ref[4 * parity + quarter].astype(jnp.float32)
        upper_half = total.astype(jnp.bfloat16)
        lower_half = (total - upper_half.astype(jnp.float32)).astype(jnp.bfloat16)
        for part in (lower_half, upper_half):
            summed = summed + jnp.dot(part, pick_ref[parity], preferred_element_type=jnp.float32)
    summed = jnp.where(inside_ref[...] > 0.0, summed, 0.0).astype(jnp.bfloat16)
    for tap in range(9):
        tap_ref[tap] = lax.dot_general(summed, upper_ref[tap], NT, preferred_element_type=jnp.float32)

    spare = jnp.zeros((cols, 256 - outs), jnp.float32)
    for frame in range(frames):
        for row in range(rows):
            for low in range(2):
                lines = []
                for dx in range(3):
                    line = up_bias_ref[...] if dx == 1 else 0.0
                    for dy in range(3):
                        at = row + (low + dy - 1) // 2
                        if 0 <= at < rows:
                            at = (frame * rows + at) * wide
                            line = line + tap_ref[3 * dy + dx, at : at + wide, :]
                    lines.append(line)
                left = lines[0][0:cols] + (lines[1] + lines[2])[1 : 1 + cols]
                right = (lines[0] + lines[1])[1 : 1 + cols] + lines[2][2 : 2 + cols]
                for side, value in ((0, left), (1, right)):
                    fine_ref[0, pl.ds(side, cols, stride=2), :] = value[:, :128]
                    fine_ref[1, pl.ds(side, cols, stride=2), :] = jnp.concatenate([value[:, 128:], spare], axis=1)
                at = (frame * fine_rows + 2 * row + low) * fine_cols
                all_ref[at : at + fine_cols, 0:128] = fine_ref[0].astype(jnp.bfloat16)
                all_ref[at : at + fine_cols, 128:256] = fine_ref[1].astype(jnp.bfloat16)
    result = jnp.dot(all_ref[...], order_ref[...], preferred_element_type=jnp.float32)
    out_ref[...] = result.astype(out_ref.dtype).reshape(out_ref.shape)


def tail(parts, skip, inside, bias, pick, upper, up_bias, order, shape):
    frames, fine_rows, fine_cols, outs = shape
    vmem = pl.BlockSpec(memory_space=pltpu.VMEM)
    return pl.pallas_call(
        tail_kernel,
        out_shape=jax.ShapeDtypeStruct(shape, jnp.bfloat16),
        in_specs=[vmem] * 8,
        out_specs=vmem,
        scratch_shapes=[
            pltpu.VMEM((9, skip.shape[0], outs), jnp.float32),
            pltpu.VMEM((2, fine_cols, 128), jnp.float32),
            pltpu.VMEM((frames * fine_rows * fine_cols, 256), jnp.bfloat16),
        ],
        compiler_params=pltpu.CompilerParams(vmem_limit_bytes=40 * 1024 * 1024),
        cost_estimate=pl.CostEstimate(
            flops=2 * skip.shape[0] * upper.size, bytes_accessed=2 * upper.size, transcendentals=0
        ),
    )(parts, skip, inside, bias, pick, upper, up_bias, order)


def per_device(sizes, features, skip, norm_gain, norm_bias, conv_weight, conv_bias, up_weight, up_bias):
    frames, rows, cols, chans = features.shape
    pairs = sizes["m"]
    strips = sizes["x"] * sizes["y1"] * 4
    columns = strips * cols
    quarter = 2 * lax.axis_index("y0") + lax.axis_index("c")
    quad = lax.axis_index("x") * sizes["y1"] + lax.axis_index("y1")
    strip = 4 * quad + quarter
    even = lax.axis_index("p") == 0

    shard, up_shard = conv_weight.shape[0], up_weight.shape[0]
    outs = up_shard * 2 * pairs
    first_tap = jnp.minimum(quarter * TAPS, 27 - TAPS)
    share = up_shard // 4
    up_rows = lax.dynamic_slice_in_dim(up_weight.transpose(1, 0, 2), quarter * share, share, axis=1)
    up_rows = jnp.pad(up_rows.reshape(9 * share, chans), ((0, 2 * shard - 9 * share), (0, 0)))
    mine = jnp.concatenate(
        [
            lax.dynamic_slice_in_dim(conv_weight, first_tap, TAPS, axis=1),
            up_rows.reshape(2, shard, chans).transpose(1, 0, 2),
        ],
        axis=1,
    )
    mine, features = lax.optimization_barrier((mine, features))
    gathered = lax.all_gather(mine, "m", axis=0, tiled=True).transpose(1, 0, 2)

    other = swap(features, "p")
    eight = jnp.concatenate([jnp.where(even, features, other), jnp.where(even, other, features)], axis=0)
    back = lax.ppermute(eight[2 * frames - 2 :], "m", [(i, i + 1) for i in range(pairs - 1)])
    ten = jnp.concatenate([back, eight], axis=0)
    by_y = swap(ten, "y0")
    everyone = handed_out(local_stats(ten), TILE, strips)

    by_c = swap(jnp.stack([ten, by_y]), "c")
    held = (ten, by_c[0], by_y, by_c[1])
    head, tail_end = held[0][:, :, :2], held[0][:, :, cols - 2 :]
    for flip in range(1, 4):
        head = jnp.where(quarter == flip, held[flip][:, :, :2], head)
        tail_end = jnp.where(quarter == 3 - flip, held[flip][:, :, cols - 2 :], tail_end)
    ending, start, head, tail_end = lax.optimization_barrier(
        (skip[:, :, cols - 1 :], skip[:, :, :1], head, tail_end)
    )
    left = strip_shift(tail_end, strips, 4)
    right = strip_shift(head, strips, -4)
    skip_left = strip_shift(ending, strips, 1)
    skip_right = strip_shift(start, strips, -1)
    left, right, skip_left, skip_right = lax.optimization_barrier((left, right, skip_left, skip_right))
    skip10 = jnp.concatenate([skip_left, skip, skip_right], axis=2).reshape(-1, chans)
    column = strip * cols - 1 + jnp.arange(skip10.shape[0]) % (cols + 2)
    inside = jnp.logical_and(column >= 0, column < columns).astype(jnp.float32)[:, None]

    ready = sum(jnp.minimum(jnp.abs(a[0, 0, 0].astype(jnp.float32)), 0.0) for a in (left, right, skip_left, skip_right))
    up_rows = jnp.concatenate(
        [gathered[TAPS], gathered[TAPS + 1].reshape(pairs, shard, chans)[:, :share].reshape(pairs * share, chans)]
    )
    up_rows = jnp.pad((up_rows.astype(jnp.float32) + ready).astype(jnp.bfloat16), ((0, -up_rows.shape[0] % 16), (0, 0)))
    up_rows = jnp.stack([up_rows, swap(up_rows, "p")])
    last = (quarter == 3).astype(jnp.int32)
    place = jnp.stack([quad * 4 * cols - 2, lax.axis_index("m"), quarter, first_tap, last])
    parts = conv_partial(
        place, ten, by_y, by_c, left, right, everyone, norm_gain, norm_bias, gathered, columns
    )
    up_rows = jnp.concatenate([up_rows, swap(up_rows, "y0")])
    up_by_c = swap(up_rows, "c")

    row = jnp.arange(9 * pairs * share).reshape(9, pairs, share)
    row_of = jnp.concatenate(
        [row[:8].transpose(1, 0, 2).reshape(-1), row[8].reshape(-1)]
    )
    count = up_rows.shape[1]
    row_of = jnp.pad(row_of, (0, count - row_of.shape[0]), constant_values=-1)
    turn = (jnp.arange(count)[:, None] == row_of[None, :]).astype(jnp.bfloat16)
    upper = in_order(turn, up_rows, up_by_c, outs)

    channel = jnp.arange(chans).reshape(pairs, 2, shard).transpose(1, 0, 2).reshape(2, chans // 2)
    pick = (channel[:, :, None] == jnp.arange(chans)[None, None, :]).astype(jnp.bfloat16)
    holder = jnp.arange(8)
    parity = jnp.bitwise_xor(lax.axis_index("p"), holder % 2)
    whose = jnp.bitwise_xor(quarter, holder // 2 % 2 * 2 + holder // 4)
    out_channel = (
        (2 * jnp.arange(pairs)[None, :, None] + parity[:, None, None]) * up_shard
        + whose[:, None, None] * share
        + jnp.arange(share)[None, None, :]
    ).reshape(outs)
    order = jnp.pad(out_channel, (0, 256 - outs), constant_values=-1)[:, None] == jnp.arange(outs)[None, :]
    order = order.astype(jnp.bfloat16)
    up_bias = jnp.dot(order[:outs].astype(jnp.float32), up_bias, precision=lax.Precision.HIGHEST)[None]
    parts = lax.all_to_all(parts, TEAM, 0, 0, tiled=True)
    return tail(
        parts, skip10, inside, conv_bias[None], pick, upper, up_bias, order, (frames, 2 * rows, 2 * cols, outs)
    )


def solution(mesh):
    strips = mesh.shape["tile"]
    side = 2
    while side * side * 2 < strips:
        side *= 2
    sizes = {"m": mesh.shape["tm"] // 2, "p": 2, "x": strips // (2 * side), "y1": side // 2, "y0": 2, "c": 2}
    fine_mesh = Mesh(mesh.devices.reshape(tuple(sizes.values())), tuple(sizes))

    def body(*arrays):
        return per_device(sizes, *arrays)

    return jax.shard_map(
        body,
        mesh=fine_mesh,
        in_specs=(
            P(TIME, None, TILE, None),
            P(TIME, None, TILE, None),
            P(),
            P(),
            P(TIME, None, None),
            P(),
            P(TIME, None, None),
            P(),
        ),
        out_specs=P(TIME, None, TILE, None),
        check_vma=False,
    )
```
